32 devices in a mesh: expert: 32 (over z, y, x, core), tensor: 1.
Axes of the slice: x: 2, y: 2, z: 4, core: 2. Of those that a mesh axis runs over, the one named last changes fastest.
Arguments:
- hidden_rows: bfloat16 [2, 512, 3584], P(None, 'expert', 'tensor'), may hold values from -6 to 6
- draft_len: int32 [2, 128], P(None, 'expert'), may hold values from 1 to 4, 320 in all within a row
- expert_ids: int32 [2, 512, 8], P(None, 'expert'), may hold values from 0 to 27, all different within a row; in each aligned block of 16 rows (0 to 15, 16 to 31, ..., all dimensions but the last counted through in order) at most 6 rows name the same one
- replica: int32 [2, 512, 8], P(None, 'expert'), may hold values from 0 to 1
- route_gain: float32 [2, 512, 8], P(None, 'expert'), may hold values from 0.03 to 0.5
- slot_up: bfloat16 [32, 3584, 1024], P('expert', None, 'tensor'), may hold values from -0.09375 to 0.09375
- slot_down: bfloat16 [32, 1024, 3584], P('expert', 'tensor'), may hold values from -0.1875 to 0.1875
- shared_up: bfloat16 [3584, 1024], P(None, 'tensor'), may hold values from -0.09375 to 0.09375
- shared_down: bfloat16 [1024, 3584], P('tensor'), may hold values from -0.1875 to 0.1875
Outputs:
- mixed: bfloat16 [2, 512, 3584], P(None, 'expert', 'tensor')
The draws below stay inside these ranges and needn't reach their ends.
Inputs may be any that keep to these rules, and one draw needn't show every extreme that they name: `expert_ids`: in each step, the 16 row places of one index of expert (live or not) name any one expert at most 6 times. Only the first 4 experts have a replica slot; for the other experts the value has no effect. `draft_len`: in each step the lengths of all 128 requests sum to 320.
All inputs are finite; a program needn't handle non-finite values. No bound on the sum of `draft_len` on one device may be relied on, other than what follows from the above.
Results may differ from the reference program's by a relative error of at most 0.019.
Values may be sent and summed in bfloat16 or wider, within the bound.
A program may use at most 192 MiB of HBM per device.

```python
import math
import jax
import jax.numpy as jnp
import numpy as np
from jax import lax

D = 3584
H = 1024
HS = 1024
TOP = 8
SPAN = 4
STEPS = 2
H_PART = 1024
ROWS_DEV = 16
REQUESTS = 128
ROWS = 512
SLOTS = 32
REPLICAS = 4
EXPERTS = 28
CAP = 6
N_EXPERT = 32
N_TENSOR = 1


def plant(array, own_key, smallest, top_value):
    longest = array.shape.index(max(array.shape))
    spots = []
    for shift in (0, 1):
        where = [jax.random.randint(jax.random.fold_in(own_key, axis), (), 0, length) for axis, length in enumerate(array.shape)]
        where[longest] = (where[longest] + shift) % array.shape[longest]
        spots.append(tuple(where))
    return array.at[spots[0]].set(smallest).at[spots[1]].set(top_value)


def block_scale(rng, shape, cuts, least, top_value):
    def one(position, shards_of):
        heights = jax.random.uniform(jax.random.fold_in(jax.random.fold_in(rng, 6), position), (shards_of,), jnp.float32, least / len(cuts), top_value / len(cuts))
        return jnp.repeat(jnp.exp(heights), shape[position] // shards_of).reshape((-1,) + (1,) * (len(shape) - position - 1))

    loudness = one(*cuts[0])
    for cut in cuts[1:]:
        loudness = loudness * one(*cut)
    return loudness


def length_profile(amount, total, bound, skew):
    weights = [(1 << 20) // math.isqrt(rank ** skew) + 1 for rank in range(2, amount + 1)]
    rest, given = total - bound - (amount - 1), [1] * (amount - 1)
    while rest > 0:
        free = [i for i in range(amount - 1) if given[i] < bound]
        whole, left = sum([weights[i] for i in free]), rest
        for i in free:
            addition = min(bound - given[i], max(1, left * weights[i] // whole), rest)
            given[i] = given[i] + addition
            rest = rest - addition
    return np.array([bound] + given)


def uneven(stream_key, number_of, total, most, slope):
    if number_of == 2:
        one = jax.random.randint(stream_key, (), max(1, total - most), min(most, total - 1) + 1)
        return jnp.stack([one, total - one])
    lengths = jnp.asarray(length_profile(number_of, total, most, slope), jnp.int32)
    couples = (number_of - 1) // 2
    donor, taker = lengths[1:1 + 2 * couples:2], lengths[2:2 + 2 * couples:2]
    room = jnp.minimum(donor - 1, most - taker)
    moved = jax.random.randint(jax.random.fold_in(stream_key, 1), (couples,), 0, 1 << 20) % (room + 1)
    lengths = lengths.at[1:1 + 2 * couples:2].set(donor - moved).at[2:2 + 2 * couples:2].set(taker + moved)
    return lengths[jax.random.permutation(jax.random.fold_in(stream_key, 2), number_of)]


def deal_out(key, own, number, rows, amount, top, bound, skew):
    ranking = jax.random.permutation(key, amount)
    crowded, common = load_shares(amount, rows * top, bound, skew, True), load_shares(amount, rows * top, bound, skew, False)
    places = jnp.arange(amount)

    def named(lengths, turn):
        used = int((lengths > 0).sum())
        fixed = max(1, used // 4)
        moved = fixed + (places - fixed + turn * (used - fixed)) % max(1, amount - fixed)
        return jnp.zeros((amount,), jnp.int32).at[ranking[jnp.where(places < fixed, places, moved)]].set(jnp.asarray(lengths, jnp.int32))

    lengths = jnp.where(number % 4 == 0, named(crowded, number // 4), named(common, number - number // 4 - 1))
    mixed = jax.random.permutation(jax.random.fold_in(own, 3), amount)
    donor, receiver = mixed[0:amount // 2 * 2:2], mixed[1:amount // 2 * 2:2]
    margin = jnp.minimum(lengths[donor] - 1, bound - lengths[receiver]) // 2
    margin = jnp.where((donor == ranking[0]) | (receiver == ranking[0]) | (lengths[receiver] == 0), 0, jnp.maximum(margin, 0))
    moved = jax.random.randint(jax.random.fold_in(own, 4), (amount // 2,), 0, 1 << 20) % (margin + 1)
    lengths = lengths.at[donor].add(-moved).at[receiver].add(moved)
    members = jnp.searchsorted(jnp.cumsum(lengths), jnp.arange(rows * top), side="right").astype(jnp.int32)
    table = members.reshape(top, rows).T
    table = table[jax.random.permutation(jax.random.fold_in(own, 1), rows)]
    turn = jax.random.randint(jax.random.fold_in(own, 2), (rows, 1), 0, top)
    return jnp.take_along_axis(table, (jnp.arange(top)[None, :] + turn) % top, axis=1)


def load_shares(count, total, limit, skew, full):
    portions = [(1 << 20) // math.isqrt(grade ** skew) + 1 for grade in range(1, count + 1)]
    largest = limit if full else min(limit, max(-(-total // count), total * portions[0] // sum(portions)))
    least = 1 if total - largest >= count - 1 else 0
    holding, rest = [largest] + [least] * (count - 1), total - largest - least * (count - 1)
    while rest > 0:
        movable = [i for i in range(1, count) if holding[i] < largest] or [i for i in range(1, count) if holding[i] < limit]
        whole, budget = sum([portions[i] for i in movable]), rest
        for i in movable:
            addition = min(limit - holding[i], max(1, budget * portions[i] // whole), rest)
            holding[i] = holding[i] + addition
            rest = rest - addition
    return np.array(holding)


def gaussian(stream_key, shape, deviation, most, split=(), kind=jnp.bfloat16):
    level = block_scale(stream_key, shape, split, -0.22, 0.18) if split else 1.0
    values = jax.random.normal(stream_key, shape, jnp.float32) * deviation * level
    return jnp.minimum(jnp.maximum(values, -most), most).astype(kind)


def setup_inputs(seed: int = 0) -> dict:
    keys = jax.random.split(jax.random.key(seed), 10)
    hidden_rows = gaussian(keys[0], (STEPS, ROWS, D), 1.0, 6.0, ((1, 32),))
    draft_len = jax.vmap(lambda own: uneven(own, REQUESTS, 5 * REQUESTS // 2, SPAN, 2))(jax.random.split(keys[1], STEPS)).reshape((STEPS, REQUESTS)).astype(jnp.int32)
    expert_ids_keys = jax.random.split(jax.random.fold_in(keys[2], 1), STEPS * ROWS // ROWS_DEV)
    expert_ids_turns = jax.random.permutation(jax.random.fold_in(keys[2], 3), STEPS * ROWS // ROWS_DEV)
    expert_ids = jax.vmap(lambda own, number: deal_out(jax.random.fold_in(keys[2], 2), own, number, ROWS_DEV, EXPERTS, TOP, CAP, 2))(expert_ids_keys, expert_ids_turns).reshape((STEPS, ROWS, TOP))
    replica = plant(jax.random.randint(keys[3], (STEPS, ROWS, TOP), 0, 2), jax.random.fold_in(keys[3], 1), 0, 1).astype(jnp.int32)
    route_gain = jnp.clip(jnp.exp(math.log(0.5) - 2.8134107 * jax.random.uniform(keys[4], (STEPS, ROWS, TOP), jnp.float32) ** block_scale(keys[4], (STEPS, ROWS, TOP), ((1, 32),), -0.2, 0.2)), 0.03, 0.5)
    slot_up = gaussian(keys[5], (SLOTS, D, H), D ** -0.5, 0.09375, ((0, 32),))
    slot_down = gaussian(keys[6], (SLOTS, H, D), H ** -0.5, 0.1875, ((0, 32),))
    shared_up = gaussian(keys[7], (D, HS), D ** -0.5, 0.09375)
    shared_down = gaussian(keys[8], (HS, D), HS ** -0.5, 0.1875)
    return dict(hidden_rows=hidden_rows, draft_len=draft_len, expert_ids=expert_ids, replica=replica, route_gain=route_gain, slot_up=slot_up, slot_down=slot_down, shared_up=shared_up, shared_down=shared_down)


def reference(hidden_rows, draft_len, expert_ids, replica, route_gain, slot_up, slot_down, shared_up, shared_down):
    results = []
    room = N_EXPERT * CAP
    entries_total = ROWS * TOP
    for index in range(STEPS):
        rows_in = hidden_rows[index]
        positions = jnp.arange(ROWS, dtype=jnp.int32)
        live_mask = (positions % SPAN < draft_len[index][positions // SPAN]).astype(jnp.float32)
        chosen = expert_ids[index]
        slot_index = jnp.where((chosen < REPLICAS) & (replica[index] == 1), chosen + EXPERTS, chosen).reshape(-1).astype(jnp.int32)
        valid = jnp.broadcast_to(live_mask[:, None] > 0.5, chosen.shape).reshape(-1)
        onehot = ((slot_index[:, None] == jnp.arange(SLOTS, dtype=jnp.int32)[None, :]) & valid[:, None]).astype(jnp.int32)
        earlier = jnp.cumsum(onehot, axis=0).astype(jnp.int32) - onehot
        order_rank = jnp.sum(earlier * onehot, axis=1).astype(jnp.int32)
        target = jnp.where(valid, slot_index * room + order_rank, SLOTS * room).astype(jnp.int32)
        table = jnp.full((SLOTS * room + 1,), entries_total, jnp.int32)
        table = table.at[target].set(jnp.arange(entries_total, dtype=jnp.int32))
        table = table[:SLOTS * room].reshape(SLOTS, room)
        padded_rows = jnp.concatenate([rows_in, jnp.zeros((1, D), rows_in.dtype)], axis=0)
        flat_gain = jnp.concatenate([(route_gain[index] * live_mask[:, None]).reshape(-1), jnp.zeros((1,), jnp.float32)])

        def serve(total, slot_number):
            entries = table[slot_number]
            row_pick = (entries // TOP).astype(jnp.int32)
            picked = padded_rows[row_pick]
            hidden = jax.nn.silu(jnp.dot(picked, slot_up[slot_number], preferred_element_type=jnp.float32)).astype(jnp.bfloat16)
            parts = jnp.einsum("mth,thd->mtd", hidden.reshape(room, N_TENSOR, H_PART).astype(jnp.float32), slot_down[slot_number].reshape(N_TENSOR, H_PART, D).astype(jnp.float32))
            parts = lax.optimization_barrier(parts.astype(jnp.bfloat16)).astype(jnp.float32)
            combined = jnp.sum(parts, axis=1) * flat_gain[entries][:, None]
            return total.at[row_pick].add(combined), None

        total, _ = lax.scan(serve, jnp.zeros((ROWS + 1, D), jnp.float32), jnp.arange(SLOTS, dtype=jnp.int32))
        shared_act = jax.nn.silu(jnp.dot(rows_in, shared_up, preferred_element_type=jnp.float32)).astype(jnp.bfloat16)
        shared_out = jnp.dot(shared_act, shared_down, preferred_element_type=jnp.float32)
        results.append(((total[:ROWS] + shared_out) * live_mask[:, None]).astype(jnp.bfloat16))
    return jnp.stack(results)
```

```python
import jax
import jax.numpy as jnp
from jax import lax
from jax.sharding import PartitionSpec as P


def slot_gains(lengths, chosen, second, gains, slot_count):
    row_count = chosen.shape[1]
    span = row_count // lengths.shape[1]
    replicas = slot_count // 8
    experts_all = slot_count - replicas
    limit = jnp.repeat(lengths, span, axis=1, total_repeat_length=row_count)
    live = (jnp.arange(row_count, dtype=jnp.int32)[None] % span < limit).astype(jnp.float32)
    slot = jnp.where((chosen < replicas) & (second == 1), chosen + experts_all, chosen)
    hit = slot[..., None] == jnp.arange(slot_count, dtype=jnp.int32)
    dense = jnp.sum(jnp.where(hit, gains[..., None], 0.0), axis=2)
    return live, dense * live[..., None]


def shards(
    hidden_rows,
    draft_len,
    expert_ids,
    replica,
    route_gain,
    slot_up,
    slot_down,
    shared_up,
    shared_down,
):
    slot_count = lax.axis_size("expert")
    me = lax.axis_index("expert")
    steps, rows, _ = hidden_rows.shape
    own = lax.all_gather(hidden_rows, "tensor", axis=2, tiled=True)
    width = own.shape[2]
    live, dense = slot_gains(draft_len, expert_ids, replica, route_gain, slot_count)
    high = dense.astype(jnp.bfloat16)
    low = (dense - high.astype(jnp.float32)).astype(jnp.bfloat16)
    packed = jnp.concatenate([own, high, low], axis=2)
    routed = []
    for index in range(steps):
        everything = lax.all_gather(packed[index], "expert", axis=0, tiled=True)
        source = everything[:, :width]
        pick = jnp.arange(slot_count) == me
        both = everything[:, width:].astype(jnp.float32)
        both = both[:, :slot_count] + both[:, slot_count:]
        weight = jnp.sum(jnp.where(pick[None], both, 0.0), axis=1, keepdims=True)
        hidden = jax.nn.silu(
            jnp.dot(source, slot_up[0], preferred_element_type=jnp.float32)
        ).astype(jnp.bfloat16)
        part = jnp.dot(hidden, slot_down[0], preferred_element_type=jnp.float32)
        part = (part * weight).astype(jnp.bfloat16)
        part = lax.psum_scatter(part, "tensor", scatter_dimension=1, tiled=True)
        routed.append(lax.psum_scatter(part, "expert", scatter_dimension=0, tiled=True))
    flat = own.reshape(steps * rows, width)
    shared_act = jax.nn.silu(
        jnp.dot(flat, shared_up, preferred_element_type=jnp.float32)
    ).astype(jnp.bfloat16)
    shared_out = jnp.dot(shared_act, shared_down, preferred_element_type=jnp.float32)
    if lax.axis_size("tensor") > 1:
        shared_out = lax.psum_scatter(shared_out, "tensor", scatter_dimension=1, tiled=True)
    shared_out = shared_out.reshape(steps, rows, -1)
    total = jnp.stack(routed).astype(jnp.float32) + shared_out
    return (total * live[..., None]).astype(jnp.bfloat16)


def solution(mesh):
    return jax.shard_map(
        shards,
        mesh=mesh,
        in_specs=(
            P(None, "expert", "tensor"),
            P(None, "expert"),
            P(None, "expert", None),
            P(None, "expert", None),
            P(None, "expert", None),
            P("expert", None, "tensor"),
            P("expert", "tensor", None),
            P(None, "tensor"),
            P("tensor", None),
        ),
        out_specs=P(None, "expert", "tensor"),
        check_vma=False,
    )
```

```python
import functools
import jax
import jax.numpy as jnp
from jax import lax
from jax.experimental import pallas as pl
from jax.experimental.pallas import tpu as pltpu
from jax.sharding import PartitionSpec as P

BF = jnp.bfloat16
F32 = jnp.float32
EXTRA = 128


def mm(a, b):
    return jnp.dot(a, b, preferred_element_type=F32)


def silu(v):
    return v / (1.0 + jnp.exp(-v))


def fused(
    x_ref, live_ref, up_hbm, down_hbm, sup_hbm, sdown_hbm, out_ref,
    gat, part, swapped, from_f, from_s, from_up, from_dn, from_fin,
    up, down, sup, sdown, hid, gain, shid, shout,
    w_sem, swap_s, swap_r, zu_s, zd_s, d1_s, d2_s, ag_r, sib_s, sib_r,
    x0_s, x0_r, f_s, f_r, s_s, s_r, ru_s, ru_r, rd_s, rd_r, fin_s, fin_r,
):
    steps = gat.shape[1]
    chips = gat.shape[2]
    rows = gat.shape[4]
    half = part.shape[5]
    lines = chips // 4
    hidden_units = up.shape[1]
    me = lax.axis_index("expert")
    c = me % 2
    chip = me // 2
    x = chip % 2
    y = (chip // 2) % 2
    z = chip // 4
    d1 = x + c * (y - x)
    d2 = y + c * (x - y)
    w1 = 1 + c
    w2 = 2 - c
    turn = 1 - 2 * (z // (lines // 2))

    def chip_of(zz, a, b):
        return zz * 4 + a * w1 + b * w2

    def order(k):
        return (z + turn * k + lines) % lines

    sib = chip * 2 + (1 - c)
    above = me + 8
    below = me - 8
    n1 = chip_of(z, 1 - d1, d2) * 2 + c
    n2 = chip_of(z, d1, 1 - d2) * 2 + c

    def send(src, dst, ssem, rsem, dev):
        return pltpu.make_async_remote_copy(
            src_ref=src, dst_ref=dst, send_sem=ssem, recv_sem=rsem,
            device_id=(dev, 0), device_id_type=pl.DeviceIdType.MESH,
        )

    barrier = pltpu.get_barrier_semaphore()

    def greet(dev):
        pl.semaphore_signal(
            barrier, inc=1, device_id=(dev, 0), device_id_type=pl.DeviceIdType.MESH
        )

    loads = [
        pltpu.make_async_copy(src, dst, w_sem.at[i])
        for i, (src, dst) in enumerate(
            [(sup_hbm, sup), (sdown_hbm, sdown), (up_hbm.at[0], up), (down_hbm.at[0], down)]
        )
    ]
    loads[0].start()
    loads[1].start()
    loads[2].start()
    loads[3].start()
    for dev in (sib, n1, n2):
        greet(dev)

    @pl.when(z > 0)
    def _():
        greet(below)

    @pl.when(z < lines - 1)
    def _():
        greet(above)

    pl.semaphore_wait(barrier, 3 + jnp.minimum(z, 1) + jnp.minimum(lines - 1 - z, 1))

    def swap(s):
        return send(
            x_ref.at[1 - c, s], gat.at[1 - c, s, chip, c], swap_s.at[s], swap_r.at[s], sib
        )

    def block(s, who):
        return gat.at[c, s, who]

    def go_up(s, zz):
        b = block(s, chip_of(zz, d1, d2))
        return send(b, b, zu_s.at[s, zz], ag_r.at[s, chip_of(zz, d1, d2)], above)

    def go_dn(s, zz):
        b = block(s, chip_of(zz, d1, d2))
        return send(b, b, zd_s.at[s, zz], ag_r.at[s, chip_of(zz, d1, d2)], below)

    def go_d1(s, zz):
        b = block(s, chip_of(zz, d1, d2))
        return send(b, b, d1_s.at[s, zz], ag_r.at[s, chip_of(zz, d1, d2)], n1)

    def go_d2(s, a, zz):
        b = block(s, chip_of(zz, a, d2))
        return send(b, b, d2_s.at[s, a * lines + zz], ag_r.at[s, chip_of(zz, a, d2)], n2)

    def go_sib(s, who):
        b = block(s, who)
        return send(b, b, sib_s.at[s, who], sib_r.at[s, who], sib)

    def arrived(s, who):
        b = block(s, who)
        send(b, b, sib_s.at[s, who], ag_r.at[s, who], sib).wait_recv()

    def spread(s, zz):
        go_d1(s, zz).start()
        go_d2(s, d1, zz).start()
        go_sib(s, chip_of(zz, d1, d2)).start()

    def ag_own(s):
        swap(s).wait_recv()

        @pl.when(z < lines - 1)
        def _():
            go_up(s, z).start()

        @pl.when(z > 0)
        def _():
            go_dn(s, z).start()

        spread(s, z)

    def ag_line(s):
        for d in range(1, lines):
            @pl.when(z - d >= 0)
            def _():
                arrived(s, chip_of(z - d, d1, d2))

                @pl.when(z < lines - 1)
                def _():
                    go_up(s, z - d).start()

                spread(s, z - d)

            @pl.when(z + d < lines)
            def _():
                arrived(s, chip_of(z + d, d1, d2))

                @pl.when(z > 0)
                def _():
                    go_dn(s, z + d).start()

                spread(s, z + d)

    def ag_d1(s, k):
        zz = order(k)
        arrived(s, chip_of(zz, 1 - d1, d2))
        go_d2(s, 1 - d1, zz).start()
        go_sib(s, chip_of(zz, 1 - d1, d2)).start()

    def ag_d2(s, m):
        a = (d1 + m // lines) % 2
        who = chip_of(order(m % lines), a, 1 - d2)
        arrived(s, who)
        go_sib(s, who).start()

    def loop(n, body):
        def step(i, carry):
            body(i)
            return carry

        lax.fori_loop(0, n, step, 0)

    def ag_finish(s):
        def one(who):
            b = gat.at[1 - c, s, who]
            send(b, b, sib_s.at[s, who], sib_r.at[s, who], sib).wait_recv()

        loop(chips, one)

    def cut(i, n):
        return pl.ds(pl.multiple_of(i * n, n), n)

    def shared_up_chunk(i):
        cols = cut(i, 256)
        v = mm(x_ref[0, :, :, :half].reshape(steps * rows, half), sup[:half, cols])
        v = v + mm(x_ref[1, :, :, :half].reshape(steps * rows, half), sup[half:, cols])
        shid[:, cols] = silu(v).astype(BF)

    def shared_down_chunk(j):
        cols = cut(j, 512)
        shout[:, cols] = mm(shid[...], sdown[:, cols])

    def gains(s):
        lane = lax.broadcasted_iota(jnp.int32, (chips * 2 * rows, EXTRA), 1)
        both = gat[0, s, :, :, :, half:].astype(F32) + gat[1, s, :, :, :, half:].astype(F32)
        both = both.reshape(chips * 2 * rows, EXTRA)
        gain[...] = jnp.sum(jnp.where(lane == me, both, 0.0), axis=1, keepdims=True)

    def up_chunk(s, i):
        cols = cut(i, 256)
        v = mm(gat[0, s, :, :, :, :half].reshape(chips * 2 * rows, half), up[:half, cols])
        v = v + mm(gat[1, s, :, :, :, :half].reshape(chips * 2 * rows, half), up[half:, cols])
        hid[:, cols] = silu(v).astype(BF)

    def down_chunk(s, h, j):
        v = mm(hid[...], down[:, pl.ds(pl.multiple_of(h * half + j * 256, 256), 256)])
        v = (v * gain[...]).astype(BF)
        part[h, s, :, :, :, cut(j, 256)] = v.reshape(chips, 2, rows, 256)

    def x0(s):
        return send(part.at[1 - c, s], swapped.at[s], x0_s.at[s], x0_r.at[s], sib)

    def both_cores(s, who):
        return part[c, s, who].astype(F32) + swapped[s, who].astype(F32)

    def f_copy(s, a, zz):
        who = chip_of(zz, a, 1 - d2)
        i = a * lines + zz
        return send(part.at[c, s, who], from_f.at[s, i], f_s.at[s, i], f_r.at[s, i], n2)

    def rs_f(s, q):
        a = (1 - d1 + q // lines) % 2
        zz = order(q % lines)
        who = chip_of(zz, a, 1 - d2)
        part[c, s, who] = both_cores(s, who).astype(BF)
        f_copy(s, a, zz).start()

    def with_f(s, a, zz):
        f_copy(s, a, zz).wait_recv()
        who = chip_of(zz, a, d2)
        return both_cores(s, who) + from_f[s, a * lines + zz].astype(F32)

    def s_copy(s, zz):
        who = chip_of(zz, 1 - d1, d2)
        return send(part.at[c, s, who], from_s.at[s, zz], s_s.at[s, zz], s_r.at[s, zz], n1)

    def rs_s(s, k):
        zz = order(k)
        who = chip_of(zz, 1 - d1, d2)
        part[c, s, who] = with_f(s, 1 - d1, zz).astype(BF)
        s_copy(s, zz).start()

    def up_copy(s, zz):
        who = chip_of(zz, d1, d2)
        return send(part.at[c, s, who], from_up.at[s, zz], ru_s.at[s, zz], ru_r.at[s, zz], above)

    def dn_copy(s, zz):
        who = chip_of(zz, d1, d2)
        return send(part.at[c, s, who], from_dn.at[s, zz], rd_s.at[s, zz], rd_r.at[s, zz], below)

    def rs_z(s):
        def collect(k):
            zz = order(k)
            who = chip_of(zz, d1, d2)
            v = with_f(s, d1, zz)
            s_copy(s, zz).wait_recv()
            part[c, s, who] = (v + from_s[s, zz].astype(F32)).astype(BF)

        loop(lines, collect)
        for d in range(lines - 1, 0, -1):
            @pl.when(z + d < lines)
            def _():
                zz = z + d
                who = chip_of(zz, d1, d2)

                @pl.when(z > 0)
                def _():
                    up_copy(s, zz).wait_recv()
                    v = part[c, s, who].astype(F32) + from_up[s, zz].astype(F32)
                    part[c, s, who] = v.astype(BF)

                up_copy(s, zz).start()

            @pl.when(z - d >= 0)
            def _():
                zz = z - d
                who = chip_of(zz, d1, d2)

                @pl.when(z < lines - 1)
                def _():
                    dn_copy(s, zz).wait_recv()
                    v = part[c, s, who].astype(F32) + from_dn[s, zz].astype(F32)
                    part[c, s, who] = v.astype(BF)

                dn_copy(s, zz).start()

    def fin(s):
        return send(part.at[c, s, chip, 1 - c], from_fin.at[s], fin_s.at[s], fin_r.at[s], sib)

    def rs_own(s):
        @pl.when(z > 0)
        def _():
            up_copy(s, z).wait_recv()
            v = part[c, s, chip].astype(F32) + from_up[s, z].astype(F32)
            part[c, s, chip] = v.astype(BF)

        @pl.when(z < lines - 1)
        def _():
            dn_copy(s, z).wait_recv()
            v = part[c, s, chip].astype(F32) + from_dn[s, z].astype(F32)
            part[c, s, chip] = v.astype(BF)

        fin(s).start()

    def write(s):
        fin(s).wait_recv()
        keep = part[c, s, chip, c].astype(F32)
        other = from_fin[s].astype(F32)
        lead = jnp.where(c == 0, keep, other)
        tail = jnp.where(c == 0, other, keep)
        alive = live_ref[s, :, :1]
        mine = pl.ds(s * rows, rows)
        out_ref[s, :, :half] = ((lead + shout[mine, :half]) * alive).astype(out_ref.dtype)
        out_ref[s, :, half:] = ((tail + shout[mine, half:]) * alive).astype(out_ref.dtype)

    for s in range(steps):
        gat[c, s, chip, c] = x_ref[c, s]
        swap(s).start()
    ag_own(0)
    ag_line(0)
    loads[0].wait()

    def first(k):
        ag_d1(0, k)
        shared_up_chunk(k)

    loop(lines, first)
    ag_own(1)
    ag_line(1)
    loads[1].wait()

    def second(m):
        ag_d2(0, m)
        shared_down_chunk(m)

    loop(2 * lines - 1, second)
    ag_d2(0, 2 * lines - 1)
    ag_finish(0)
    loads[2].wait()
    gains(0)

    def third(i):
        up_chunk(0, i)
        ag_d1(1, i)

    loop(hidden_units // 256, third)
    loads[3].wait()

    def fourth(j):
        down_chunk(0, 1 - c, j)
        ag_d2(1, j)

    loop(half // 256, fourth)
    ag_d2(1, 2 * lines - 1)
    x0(0).start()
    loop(half // 256, lambda j: down_chunk(0, c, j))
    x0(0).wait_recv()
    loop(2 * lines, lambda q: rs_f(0, q))
    ag_finish(1)
    gains(1)
    loop(hidden_units // 256, lambda i: up_chunk(1, i))

    def fifth(j):
        down_chunk(1, 1 - c, j)

        @pl.when(j >= half // 256 - lines)
        def _():
            rs_s(0, j - (half // 256 - lines))

    loop(half // 256, fifth)
    x0(1).start()
    loop(half // 256, lambda j: down_chunk(1, c, j))
    x0(1).wait_recv()
    loop(2 * lines, lambda q: rs_f(1, q))
    rs_z(0)
    loop(lines, lambda k: rs_s(1, k))
    rs_own(0)
    rs_z(1)
    write(0)
    rs_own(1)
    write(1)

    for s in range(steps):
        swap(s).wait_send()
        x0(s).wait_send()
        fin(s).wait_send()

        def planes(zz):
            go_d1(s, zz).wait_send()
            go_d2(s, 0, zz).wait_send()
            go_d2(s, 1, zz).wait_send()
            f_copy(s, 0, zz).wait_send()
            f_copy(s, 1, zz).wait_send()
            s_copy(s, zz).wait_send()

            @pl.when((zz <= z) & (z < lines - 1))
            def _():
                go_up(s, zz).wait_send()

            @pl.when((zz >= z) & (z > 0))
            def _():
                go_dn(s, zz).wait_send()

            @pl.when(zz > z)
            def _():
                up_copy(s, zz).wait_send()

            @pl.when(zz < z)
            def _():
                dn_copy(s, zz).wait_send()

        loop(lines, planes)
        loop(chips, lambda who: go_sib(s, who).wait_send())


def fused_layer(
    hidden_rows, draft_len, expert_ids, replica, route_gain, slot_up, slot_down, shared_up, shared_down
):
    slot_count = lax.axis_size("expert")
    steps, rows, width = hidden_rows.shape
    half = width // 2
    chips = slot_count // 2
    lines = chips // 4
    hidden_units = slot_up.shape[2]
    live, dense = slot_gains(draft_len, expert_ids, replica, route_gain, slot_count)
    high = dense.astype(BF)
    low = (dense - high.astype(F32)).astype(BF)
    tail = jnp.pad(jnp.stack([high, low]), ((0, 0), (0, 0), (0, 0), (0, EXTRA - slot_count)))
    halves = jnp.stack([hidden_rows[..., :half], hidden_rows[..., half:]])
    packed = jnp.concatenate([halves, tail], axis=3)
    alive = jnp.broadcast_to(live[..., None], (steps, rows, 128))
    vm = pl.BlockSpec(memory_space=pltpu.VMEM)
    hbm = pl.BlockSpec(memory_space=pl.ANY)
    dma = pltpu.SemaphoreType.DMA
    flops = 4 * steps * rows * (slot_count + 1) * width * hidden_units
    return pl.pallas_call(
        fused,
        out_shape=jax.ShapeDtypeStruct((steps, rows, width), BF),
        in_specs=[vm, vm, hbm, hbm, hbm, hbm],
        out_specs=vm,
        scratch_shapes=[
            pltpu.VMEM((2, steps, chips, 2, rows, half + EXTRA), BF),
            pltpu.VMEM((2, steps, chips, 2, rows, half), BF),
            pltpu.VMEM((steps, chips, 2, rows, half), BF),
            pltpu.VMEM((steps, 2 * lines, 2, rows, half), BF),
            pltpu.VMEM((steps, lines, 2, rows, half), BF),
            pltpu.VMEM((steps, lines, 2, rows, half), BF),
            pltpu.VMEM((steps, lines, 2, rows, half), BF),
            pltpu.VMEM((steps, rows, half), BF),
            pltpu.VMEM(slot_up.shape[1:], BF),
            pltpu.VMEM(slot_down.shape[1:], BF),
            pltpu.VMEM(shared_up.shape, BF),
            pltpu.VMEM(shared_down.shape, BF),
            pltpu.VMEM((slot_count * rows, hidden_units), BF),
            pltpu.VMEM((slot_count * rows, 1), F32),
            pltpu.VMEM((steps * rows, shared_up.shape[1]), BF),
            pltpu.VMEM((steps * rows, width), F32),
            dma((4,)), dma((steps,)), dma((steps,)),
            dma((steps, lines)), dma((steps, lines)), dma((steps, lines)),
            dma((steps, 2 * lines)), dma((steps, chips)),
            dma((steps, chips)), dma((steps, chips)),
            dma((steps,)), dma((steps,)),
            dma((steps, 2 * lines)), dma((steps, 2 * lines)),
            dma((steps, lines)), dma((steps, lines)),
            dma((steps, lines)), dma((steps, lines)),
            dma((steps, lines)), dma((steps, lines)),
            dma((steps,)), dma((steps,)),
        ],
        compiler_params=pltpu.CompilerParams(
            collective_id=0, has_side_effects=True, vmem_limit_bytes=62 * 1024 * 1024
        ),
        cost_estimate=pl.CostEstimate(
            flops=flops, bytes_accessed=4 * 2 * width * hidden_units, transcendentals=0
        ),
        name="fused_layer",
    )(packed, alive, slot_up, slot_down, shared_up, shared_down)


def slot_gains(lengths, chosen, second, gains, slot_count):
    row_count = chosen.shape[1]
    span = row_count // lengths.shape[1]
    replicas = slot_count // 8
    experts_all = slot_count - replicas
    limit = jnp.repeat(lengths, span, axis=1, total_repeat_length=row_count)
    live = (jnp.arange(row_count, dtype=jnp.int32)[None] % span < limit).astype(jnp.float32)
    slot = jnp.where((chosen < replicas) & (second == 1), chosen + experts_all, chosen)
    hit = slot[..., None] == jnp.arange(slot_count, dtype=jnp.int32)
    dense = jnp.sum(jnp.where(hit, gains[..., None], 0.0), axis=2)
    return live, dense * live[..., None]


def shards(
    hidden_rows,
    draft_len,
    expert_ids,
    replica,
    route_gain,
    slot_up,
    slot_down,
    shared_up,
    shared_down,
):
    slot_count = lax.axis_size("expert")
    me = lax.axis_index("expert")
    steps, rows, _ = hidden_rows.shape
    own = lax.all_gather(hidden_rows, "tensor", axis=2, tiled=True)
    width = own.shape[2]
    live, dense = slot_gains(draft_len, expert_ids, replica, route_gain, slot_count)
    high = dense.astype(jnp.bfloat16)
    low = (dense - high.astype(jnp.float32)).astype(jnp.bfloat16)
    packed = jnp.concatenate([own, high, low], axis=2)
    routed = []
    for index in range(steps):
        everything = lax.all_gather(packed[index], "expert", axis=0, tiled=True)
        source = everything[:, :width]
        pick = jnp.arange(slot_count) == me
        both = everything[:, width:].astype(jnp.float32)
        both = both[:, :slot_count] + both[:, slot_count:]
        weight = jnp.sum(jnp.where(pick[None], both, 0.0), axis=1, keepdims=True)
        hidden = jax.nn.silu(
            jnp.dot(source, slot_up[0], preferred_element_type=jnp.float32)
        ).astype(jnp.bfloat16)
        part = jnp.dot(hidden, slot_down[0], preferred_element_type=jnp.float32)
        part = (part * weight).astype(jnp.bfloat16)
        part = lax.psum_scatter(part, "tensor", scatter_dimension=1, tiled=True)
        routed.append(lax.psum_scatter(part, "expert", scatter_dimension=0, tiled=True))
    flat = own.reshape(steps * rows, width)
    shared_act = jax.nn.silu(
        jnp.dot(flat, shared_up, preferred_element_type=jnp.float32)
    ).astype(jnp.bfloat16)
    shared_out = jnp.dot(shared_act, shared_down, preferred_element_type=jnp.float32)
    if lax.axis_size("tensor") > 1:
        shared_out = lax.psum_scatter(shared_out, "tensor", scatter_dimension=1, tiled=True)
    shared_out = shared_out.reshape(steps, rows, -1)
    total = jnp.stack(routed).astype(jnp.float32) + shared_out
    return (total * live[..., None]).astype(jnp.bfloat16)


def solution(mesh):
    fits = mesh.shape["tensor"] == 1 and mesh.shape["expert"] == 32
    return jax.shard_map(
        fused_layer if fits else shards,
        mesh=mesh,
        in_specs=(
            P(None, "expert", "tensor"),
            P(None, "expert"),
            P(None, "expert", None),
            P(None, "expert", None),
            P(None, "expert", None),
            P("expert", None, "tensor"),
            P("expert", "tensor", None),
            P(None, "tensor"),
            P("tensor", None),
        ),
        out_specs=P(None, "expert", "tensor"),
        check_vma=False,
    )
```

```python
import functools
import jax
import jax.numpy as jnp
from jax import lax
from jax.experimental import pallas as pl
from jax.experimental.pallas import tpu as pltpu
from jax.sharding import PartitionSpec as P

BF = jnp.bfloat16
F32 = jnp.float32
EXTRA = 128


def mm(a, b):
    return jnp.dot(a, b, preferred_element_type=F32)


def silu(v):
    return v / (1.0 + jnp.exp(-v))


def fused(
    own_ref, len_ref, ids_ref, second_ref, gain_ref, up_hbm, down_hbm, sup_hbm, sdown_hbm,
    out_ref, x_ref, live_ref, gat, part, swapped, from_f, from_s, from_up, from_dn, from_fin,
    up, down, sup, sdown, hid, gain, shid, shout,
    w_sem, swap_s, swap_r, zu_s, zd_s, d1_s, d2_s, ag_r, sib_s, sib_r,
    x0_s, x0_r, f_s, f_r, s_s, s_r, ru_s, ru_r, rd_s, rd_r, fin_s, fin_r,
):
    steps = gat.shape[1]
    chips = gat.shape[2]
    rows = gat.shape[4]
    half = part.shape[5]
    lines = chips // 4
    hidden_units = up.shape[1]
    me = lax.axis_index("expert")
    c = me % 2
    chip = me // 2
    x = chip % 2
    y = (chip // 2) % 2
    z = chip // 4
    d1 = x + c * (y - x)
    d2 = y + c * (x - y)
    w1 = 1 + c
    w2 = 2 - c
    turn = 1 - 2 * (z // (lines // 2))

    def chip_of(zz, a, b):
        return zz * 4 + a * w1 + b * w2

    def order(k):
        return (z + turn * k + lines) % lines

    sib = chip * 2 + (1 - c)
    above = me + 8
    below = me - 8
    n1 = chip_of(z, 1 - d1, d2) * 2 + c
    n2 = chip_of(z, d1, 1 - d2) * 2 + c

    def send(src, dst, ssem, rsem, dev):
        return pltpu.make_async_remote_copy(
            src_ref=src, dst_ref=dst, send_sem=ssem, recv_sem=rsem,
            device_id=(dev, 0), device_id_type=pl.DeviceIdType.MESH,
        )

    barrier = pltpu.get_barrier_semaphore()

    def greet(dev):
        pl.semaphore_signal(
            barrier, inc=1, device_id=(dev, 0), device_id_type=pl.DeviceIdType.MESH
        )

    loads = [
        pltpu.make_async_copy(src, dst, w_sem.at[i])
        for i, (src, dst) in enumerate(
            [(sup_hbm, sup), (sdown_hbm, sdown), (up_hbm.at[0], up), (down_hbm.at[0], down)]
        )
    ]
    loads[0].start()
    loads[1].start()
    loads[2].start()
    loads[3].start()
    for dev in (sib, n1, n2):
        greet(dev)

    @pl.when(z > 0)
    def _():
        greet(below)

    @pl.when(z < lines - 1)
    def _():
        greet(above)

    slot_count = chips * 2
    replicas = slot_count // 8
    spans = len_ref.shape[1]
    span = rows // spans
    row_at = lax.broadcasted_iota(jnp.int32, (rows, spans), 0)
    start_at = lax.broadcasted_iota(jnp.int32, (rows, spans), 1) * span
    lane_at = lax.broadcasted_iota(jnp.int32, (rows, EXTRA), 1)
    for s in range(steps):
        lens = jnp.minimum(len_ref[pl.ds(s, 1), :], span)
        inside = (row_at >= start_at) & (row_at < start_at + lens)
        alive = jnp.sum(jnp.where(inside, 1.0, 0.0), axis=1, keepdims=True)
        ids = ids_ref[s]
        moved = (ids < replicas) & (second_ref[s] == 1)
        slot = jnp.where(moved, ids + (slot_count - replicas), ids)
        weights = gain_ref[s]
        dense = jnp.zeros((rows, EXTRA), F32)
        for k in range(ids.shape[1]):
            dense = dense + jnp.where(lane_at == slot[:, k : k + 1], weights[:, k : k + 1], 0.0)
        dense = dense * alive
        high = dense.astype(BF)
        x_ref[0, s, :, :half] = own_ref[s, :, :half]
        x_ref[1, s, :, :half] = own_ref[s, :, half:]
        x_ref[0, s, :, half:] = high
        x_ref[1, s, :, half:] = (dense - high.astype(F32)).astype(BF)
        live_ref[s] = jnp.broadcast_to(alive, (rows, 128))

    pl.semaphore_wait(barrier, 3 + jnp.minimum(z, 1) + jnp.minimum(lines - 1 - z, 1))

    def swap(s):
        return send(
            x_ref.at[1 - c, s], gat.at[1 - c, s, chip, c], swap_s.at[s], swap_r.at[s], sib
        )

    def block(s, who):
        return gat.at[c, s, who]

    def go_up(s, zz):
        b = block(s, chip_of(zz, d1, d2))
        return send(b, b, zu_s.at[s, zz], ag_r.at[s, chip_of(zz, d1, d2)], above)

    def go_dn(s, zz):
        b = block(s, chip_of(zz, d1, d2))
        return send(b, b, zd_s.at[s, zz], ag_r.at[s, chip_of(zz, d1, d2)], below)

    def go_d1(s, zz):
        b = block(s, chip_of(zz, d1, d2))
        return send(b, b, d1_s.at[s, zz], ag_r.at[s, chip_of(zz, d1, d2)], n1)

    def go_d2(s, a, zz):
        b = block(s, chip_of(zz, a, d2))
        return send(b, b, d2_s.at[s, a * lines + zz], ag_r.at[s, chip_of(zz, a, d2)], n2)

    def go_sib(s, who):
        b = block(s, who)
        return send(b, b, sib_s.at[s, who], sib_r.at[s, who], sib)

    def arrived(s, who):
        b = block(s, who)
        send(b, b, sib_s.at[s, who], ag_r.at[s, who], sib).wait_recv()

    def spread(s, zz):
        go_d1(s, zz).start()
        go_d2(s, d1, zz).start()
        go_sib(s, chip_of(zz, d1, d2)).start()

    def ag_own(s):
        swap(s).wait_recv()

        @pl.when(z < lines - 1)
        def _():
            go_up(s, z).start()

        @pl.when(z > 0)
        def _():
            go_dn(s, z).start()

        spread(s, z)

    def ag_line(s):
        for d in range(1, lines):
            @pl.when(z - d >= 0)
            def _():
                arrived(s, chip_of(z - d, d1, d2))

                @pl.when(z < lines - 1)
                def _():
                    go_up(s, z - d).start()

                spread(s, z - d)

            @pl.when(z + d < lines)
            def _():
                arrived(s, chip_of(z + d, d1, d2))

                @pl.when(z > 0)
                def _():
                    go_dn(s, z + d).start()

                spread(s, z + d)

    def ag_d1(s, k):
        zz = order(k)
        arrived(s, chip_of(zz, 1 - d1, d2))
        go_d2(s, 1 - d1, zz).start()
        go_sib(s, chip_of(zz, 1 - d1, d2)).start()

    def ag_d2(s, m):
        a = (d1 + m // lines) % 2
        who = chip_of(order(m % lines), a, 1 - d2)
        arrived(s, who)
        go_sib(s, who).start()

    def loop(n, body):
        def step(i, carry):
            body(i)
            return carry

        lax.fori_loop(0, n, step, 0)

    def ag_finish(s):
        def one(who):
            b = gat.at[1 - c, s, who]
            send(b, b, sib_s.at[s, who], sib_r.at[s, who], sib).wait_recv()

        loop(chips, one)

    def cut(i, n):
        return pl.ds(pl.multiple_of(i * n, n), n)

    def shared_up_chunk(i):
        cols = cut(i, 256)
        v = mm(x_ref[0, :, :, :half].reshape(steps * rows, half), sup[:half, cols])
        v = v + mm(x_ref[1, :, :, :half].reshape(steps * rows, half), sup[half:, cols])
        shid[:, cols] = silu(v).astype(BF)

    def shared_down_chunk(j):
        cols = cut(j, 512)
        shout[:, cols] = mm(shid[...], sdown[:, cols])

    def gains(s):
        lane = lax.broadcasted_iota(jnp.int32, (chips * 2 * rows, EXTRA), 1)
        both = gat[0, s, :, :, :, half:].astype(F32) + gat[1, s, :, :, :, half:].astype(F32)
        both = both.reshape(chips * 2 * rows, EXTRA)
        mine = jnp.sum(jnp.where(lane == me, both, 0.0), axis=1, keepdims=True)
        gain[...] = mine.reshape(chips, 2 * rows, 1)

    def up_chunk(s, i):
        cols = cut(i, 256)
        v = mm(gat[0, s, :, :, :, :half].reshape(chips * 2 * rows, half), up[:half, cols])
        v = v + mm(gat[1, s, :, :, :, :half].reshape(chips * 2 * rows, half), up[half:, cols])
        hid[:, :, cols] = silu(v).astype(BF).reshape(chips, 2 * rows, 256)

    def members(t, far):
        there = y + t * (x - y)
        b = (1 - there) if far else there
        return [
            zz * 4 + a * (1 + t) + b * (2 - t) for zz in range(lines) for a in range(2)
        ]

    def down_chunk(s, t, far, j):
        group = members(t, far)
        source = jnp.concatenate([hid[who] for who in group], axis=0)
        scale = jnp.concatenate([gain[who] for who in group], axis=0)
        v = mm(source, down[:, pl.ds(pl.multiple_of(t * half + j * 256, 256), 256)])
        v = (v * scale).astype(BF).reshape(len(group), 2, rows, 256)
        for i, who in enumerate(group):
            part[t, s, who, :, :, cut(j, 256)] = v[i]

    def x0(s, who):
        return send(
            part.at[1 - c, s, who], swapped.at[s, who], x0_s.at[s, who], x0_r.at[s, who], sib
        )

    def x0_start(s, far):
        for who in members(1 - c, far):
            x0(s, who).start()

    def both_cores(s, who):
        x0(s, who).wait_recv()
        return part[c, s, who].astype(F32) + swapped[s, who].astype(F32)

    def f_copy(s, a, zz):
        who = chip_of(zz, a, 1 - d2)
        i = a * lines + zz
        return send(part.at[c, s, who], from_f.at[s, i], f_s.at[s, i], f_r.at[s, i], n2)

    def rs_f(s, q):
        a = (1 - d1 + q // lines) % 2
        zz = order(q % lines)
        who = chip_of(zz, a, 1 - d2)
        part[c, s, who] = both_cores(s, who).astype(BF)
        f_copy(s, a, zz).start()

    def with_f(s, a, zz):
        f_copy(s, a, zz).wait_recv()
        who = chip_of(zz, a, d2)
        return both_cores(s, who) + from_f[s, a * lines + zz].astype(F32)

    def s_copy(s, zz):
        who = chip_of(zz, 1 - d1, d2)
        return send(part.at[c, s, who], from_s.at[s, zz], s_s.at[s, zz], s_r.at[s, zz], n1)

    def rs_s(s, k):
        zz = order(k)
        who = chip_of(zz, 1 - d1, d2)
        part[c, s, who] = with_f(s, 1 - d1, zz).astype(BF)
        s_copy(s, zz).start()

    def up_copy(s, zz):
        who = chip_of(zz, d1, d2)
        return send(part.at[c, s, who], from_up.at[s, zz], ru_s.at[s, zz], ru_r.at[s, zz], above)

    def dn_copy(s, zz):
        who = chip_of(zz, d1, d2)
        return send(part.at[c, s, who], from_dn.at[s, zz], rd_s.at[s, zz], rd_r.at[s, zz], below)

    def rs_z(s):
        def collect(k):
            zz = order(k)
            who = chip_of(zz, d1, d2)
            v = with_f(s, d1, zz)
            s_copy(s, zz).wait_recv()
            part[c, s, who] = (v + from_s[s, zz].astype(F32)).astype(BF)

        loop(lines, collect)
        for d in range(lines - 1, 0, -1):
            @pl.when(z + d < lines)
            def _():
                zz = z + d
                who = chip_of(zz, d1, d2)

                @pl.when(z > 0)
                def _():
                    up_copy(s, zz).wait_recv()
                    v = part[c, s, who].astype(F32) + from_up[s, zz].astype(F32)
                    part[c, s, who] = v.astype(BF)

                up_copy(s, zz).start()

            @pl.when(z - d >= 0)
            def _():
                zz = z - d
                who = chip_of(zz, d1, d2)

                @pl.when(z < lines - 1)
                def _():
                    dn_copy(s, zz).wait_recv()
                    v = part[c, s, who].astype(F32) + from_dn[s, zz].astype(F32)
                    part[c, s, who] = v.astype(BF)

                dn_copy(s, zz).start()

    def fin(s):
        return send(part.at[c, s, chip, 1 - c], from_fin.at[s], fin_s.at[s], fin_r.at[s], sib)

    def rs_own(s):
        @pl.when(z > 0)
        def _():
            up_copy(s, z).wait_recv()
            v = part[c, s, chip].astype(F32) + from_up[s, z].astype(F32)
            part[c, s, chip] = v.astype(BF)

        @pl.when(z < lines - 1)
        def _():
            dn_copy(s, z).wait_recv()
            v = part[c, s, chip].astype(F32) + from_dn[s, z].astype(F32)
            part[c, s, chip] = v.astype(BF)

        fin(s).start()

    def write(s):
        fin(s).wait_recv()
        keep = part[c, s, chip, c].astype(F32)
        other = from_fin[s].astype(F32)
        lead = jnp.where(c == 0, keep, other)
        tail = jnp.where(c == 0, other, keep)
        alive = live_ref[s, :, :1]
        mine = pl.ds(s * rows, rows)
        out_ref[s, :, :half] = ((lead + shout[mine, :half]) * alive).astype(out_ref.dtype)
        out_ref[s, :, half:] = ((tail + shout[mine, half:]) * alive).astype(out_ref.dtype)

    for s in range(steps):
        gat[c, s, chip, c] = x_ref[c, s]
        swap(s).start()
    ag_own(0)
    ag_line(0)
    loads[0].wait()

    def first(k):
        ag_d1(0, k)
        shared_up_chunk(k)

    loop(lines, first)
    ag_own(1)
    ag_line(1)
    loads[1].wait()

    def second(m):
        ag_d2(0, m)
        shared_down_chunk(m)

    loop(2 * lines - 1, second)
    ag_d2(0, 2 * lines - 1)
    ag_finish(0)
    loads[2].wait()
    gains(0)

    def third(i):
        up_chunk(0, i)
        ag_d1(1, i)

    loop(hidden_units // 256, third)
    loads[3].wait()
    chunks = half // 256
    late = chunks - lines
    loop(chunks, lambda j: down_chunk(0, 1 - c, True, j))
    x0_start(0, True)
    loop(chunks, lambda j: down_chunk(0, c, True, j))
    loop(2 * lines, lambda q: rs_f(0, q))

    def fourth(j):
        down_chunk(0, 1 - c, False, j)

        @pl.when(j >= late)
        def _():
            ag_d2(1, j - late)

    loop(chunks, fourth)
    x0_start(0, False)

    def fifth(j):
        down_chunk(0, c, False, j)

        @pl.when(j >= late)
        def _():
            ag_d2(1, j - late + lines)

    loop(chunks, fifth)
    ag_finish(1)
    gains(1)
    loop(hidden_units // 256, lambda i: up_chunk(1, i))

    def sixth(j):
        down_chunk(1, 1 - c, True, j)

        @pl.when(j >= late)
        def _():
            rs_s(0, j - late)

    loop(chunks, sixth)
    x0_start(1, True)
    loop(chunks, lambda j: down_chunk(1, c, True, j))
    loop(2 * lines, lambda q: rs_f(1, q))
    loop(chunks, lambda j: down_chunk(1, 1 - c, False, j))
    x0_start(1, False)
    loop(chunks, lambda j: down_chunk(1, c, False, j))
    rs_z(0)
    loop(lines, lambda k: rs_s(1, k))
    rs_own(0)
    rs_z(1)
    write(0)
    rs_own(1)
    write(1)

    for s in range(steps):
        swap(s).wait_send()
        fin(s).wait_send()

        def planes(zz):
            go_d1(s, zz).wait_send()
            go_d2(s, 0, zz).wait_send()
            go_d2(s, 1, zz).wait_send()
            f_copy(s, 0, zz).wait_send()
            f_copy(s, 1, zz).wait_send()
            s_copy(s, zz).wait_send()

            @pl.when((zz <= z) & (z < lines - 1))
            def _():
                go_up(s, zz).wait_send()

            @pl.when((zz >= z) & (z > 0))
            def _():
                go_dn(s, zz).wait_send()

            @pl.when(zz > z)
            def _():
                up_copy(s, zz).wait_send()

            @pl.when(zz < z)
            def _():
                dn_copy(s, zz).wait_send()

        loop(lines, planes)

        def siblings(who):
            go_sib(s, who).wait_send()
            x0(s, who).wait_send()

        loop(chips, siblings)


def fused_layer(
    hidden_rows, draft_len, expert_ids, replica, route_gain, slot_up, slot_down, shared_up, shared_down
):
    slot_count = lax.axis_size("expert")
    steps, rows, width = hidden_rows.shape
    half = width // 2
    chips = slot_count // 2
    lines = chips // 4
    hidden_units = slot_up.shape[2]
    vm = pl.BlockSpec(memory_space=pltpu.VMEM)
    hbm = pl.BlockSpec(memory_space=pl.ANY)
    dma = pltpu.SemaphoreType.DMA
    flops = 4 * steps * rows * (slot_count + 1) * width * hidden_units
    return pl.pallas_call(
        fused,
        out_shape=jax.ShapeDtypeStruct((steps, rows, width), BF),
        in_specs=[vm] * 5 + [hbm] * 4,
        out_specs=vm,
        scratch_shapes=[
            pltpu.VMEM((2, steps, rows, half + EXTRA), BF),
            pltpu.VMEM((steps, rows, 128), F32),
            pltpu.VMEM((2, steps, chips, 2, rows, half + EXTRA), BF),
            pltpu.VMEM((2, steps, chips, 2, rows, half), BF),
            pltpu.VMEM((steps, chips, 2, rows, half), BF),
            pltpu.VMEM((steps, 2 * lines, 2, rows, half), BF),
            pltpu.VMEM((steps, lines, 2, rows, half), BF),
            pltpu.VMEM((steps, lines, 2, rows, half), BF),
            pltpu.VMEM((steps, lines, 2, rows, half), BF),
            pltpu.VMEM((steps, rows, half), BF),
            pltpu.VMEM(slot_up.shape[1:], BF),
            pltpu.VMEM(slot_down.shape[1:], BF),
            pltpu.VMEM(shared_up.shape, BF),
            pltpu.VMEM(shared_down.shape, BF),
            pltpu.VMEM((chips, 2 * rows, hidden_units), BF),
            pltpu.VMEM((chips, 2 * rows, 1), F32),
            pltpu.VMEM((steps * rows, shared_up.shape[1]), BF),
            pltpu.VMEM((steps * rows, width), F32),
            dma((4,)), dma((steps,)), dma((steps,)),
            dma((steps, lines)), dma((steps, lines)), dma((steps, lines)),
            dma((steps, 2 * lines)), dma((steps, chips)),
            dma((steps, chips)), dma((steps, chips)),
            dma((steps, chips)), dma((steps, chips)),
            dma((steps, 2 * lines)), dma((steps, 2 * lines)),
            dma((steps, lines)), dma((steps, lines)),
            dma((steps, lines)), dma((steps, lines)),
            dma((steps, lines)), dma((steps, lines)),
            dma((steps,)), dma((steps,)),
        ],
        compiler_params=pltpu.CompilerParams(
            collective_id=0, has_side_effects=True, vmem_limit_bytes=62 * 1024 * 1024
        ),
        cost_estimate=pl.CostEstimate(
            flops=flops, bytes_accessed=4 * 2 * width * hidden_units, transcendentals=0
        ),
        name="fused_layer",
    )(
        hidden_rows, draft_len, expert_ids, replica, route_gain,
        slot_up, slot_down, shared_up, shared_down,
    )


def slot_gains(lengths, chosen, second, gains, slot_count):
    row_count = chosen.shape[1]
    span = row_count // lengths.shape[1]
    replicas = slot_count // 8
    experts_all = slot_count - replicas
    limit = jnp.repeat(lengths, span, axis=1, total_repeat_length=row_count)
    live = (jnp.arange(row_count, dtype=jnp.int32)[None] % span < limit).astype(jnp.float32)
    slot = jnp.where((chosen < replicas) & (second == 1), chosen + experts_all, chosen)
    hit = slot[..., None] == jnp.arange(slot_count, dtype=jnp.int32)
    dense = jnp.sum(jnp.where(hit, gains[..., None], 0.0), axis=2)
    return live, dense * live[..., None]


def shards(
    hidden_rows,
    draft_len,
    expert_ids,
    replica,
    route_gain,
    slot_up,
    slot_down,
    shared_up,
    shared_down,
):
    slot_count = lax.axis_size("expert")
    me = lax.axis_index("expert")
    steps, rows, _ = hidden_rows.shape
    own = lax.all_gather(hidden_rows, "tensor", axis=2, tiled=True)
    width = own.shape[2]
    live, dense = slot_gains(draft_len, expert_ids, replica, route_gain, slot_count)
    high = dense.astype(jnp.bfloat16)
    low = (dense - high.astype(jnp.float32)).astype(jnp.bfloat16)
    packed = jnp.concatenate([own, high, low], axis=2)
    routed = []
    for index in range(steps):
        everything = lax.all_gather(packed[index], "expert", axis=0, tiled=True)
        source = everything[:, :width]
        pick = jnp.arange(slot_count) == me
        both = everything[:, width:].astype(jnp.float32)
        both = both[:, :slot_count] + both[:, slot_count:]
        weight = jnp.sum(jnp.where(pick[None], both, 0.0), axis=1, keepdims=True)
        hidden = jax.nn.silu(
            jnp.dot(source, slot_up[0], preferred_element_type=jnp.float32)
        ).astype(jnp.bfloat16)
        part = jnp.dot(hidden, slot_down[0], preferred_element_type=jnp.float32)
        part = (part * weight).astype(jnp.bfloat16)
        part = lax.psum_scatter(part, "tensor", scatter_dimension=1, tiled=True)
        routed.append(lax.psum_scatter(part, "expert", scatter_dimension=0, tiled=True))
    flat = own.reshape(steps * rows, width)
    shared_act = jax.nn.silu(
        jnp.dot(flat, shared_up, preferred_element_type=jnp.float32)
    ).astype(jnp.bfloat16)
    shared_out = jnp.dot(shared_act, shared_down, preferred_element_type=jnp.float32)
    if lax.axis_size("tensor") > 1:
        shared_out = lax.psum_scatter(shared_out, "tensor", scatter_dimension=1, tiled=True)
    shared_out = shared_out.reshape(steps, rows, -1)
    total = jnp.stack(routed).astype(jnp.float32) + shared_out
    return (total * live[..., None]).astype(jnp.bfloat16)


def solution(mesh):
    fits = mesh.shape["tensor"] == 1 and mesh.shape["expert"] == 32
    return jax.shard_map(
        fused_layer if fits else shards,
        mesh=mesh,
        in_specs=(
            P(None, "expert", "tensor"),
            P(None, "expert"),
            P(None, "expert", None),
            P(None, "expert", None),
            P(None, "expert", None),
            P("expert", None, "tensor"),
            P("expert", "tensor", None),
            P(None, "tensor"),
            P("tensor", None),
        ),
        out_specs=P(None, "expert", "tensor"),
        check_vma=False,
    )
```

```python
import functools
import jax
import jax.numpy as jnp
from jax import lax
from jax.experimental import pallas as pl
from jax.experimental.pallas import tpu as pltpu
from jax.sharding import PartitionSpec as P

BF = jnp.bfloat16
F32 = jnp.float32
EXTRA = 128


def mm(a, b):
    return jnp.dot(a, b, preferred_element_type=F32)


def silu(v):
    return v / (1.0 + jnp.exp(-v))


def fused(
    own_ref, len_ref, ids_ref, second_ref, gain_ref, up_hbm, down_hbm, sup_hbm, sdown_hbm,
    out_ref, x_ref, live_ref, gat, part, swapped, from_f, from_c, from_s, from_up, from_dn, from_fin,
    up, down, sup, sdown, hid, gain, shid, shout,
    w_sem, swap_s, swap_r, zu_s, zd_s, d1_s, d2_s, ag_r, sib_s, sib_r,
    x0_s, x0_r, f_s, f_r, s_s, s_r, ru_s, ru_r, rd_s, rd_r, fin_s, fin_r, cx_s, c_s, c_r,
):
    steps = gat.shape[1]
    chips = gat.shape[2]
    rows = gat.shape[4]
    half = part.shape[5]
    lines = chips // 4
    hidden_units = up.shape[1]
    me = lax.axis_index("expert")
    c = me % 2
    chip = me // 2
    x = chip % 2
    y = (chip // 2) % 2
    z = chip // 4
    d1 = x + c * (y - x)
    d2 = y + c * (x - y)
    w1 = 1 + c
    w2 = 2 - c
    upper = z // 2
    inner = (z + 1) // 2 == 1
    turn = 1 - 2 * upper

    def chip_of(zz, a, b):
        return zz * 4 + a * w1 + b * w2

    def same(k):
        return z + k * (4 * upper + 1 - 2 * z)

    def other(k):
        return 2 + k - upper * (1 + 2 * k)

    def order(k):
        return (z + turn * k + lines) % lines

    sib = chip * 2 + (1 - c)
    above = me + 8
    below = me - 8
    toward = me + 8 * turn
    away = me - 8 * turn
    n1 = chip_of(z, 1 - d1, d2) * 2 + c
    n2 = chip_of(z, d1, 1 - d2) * 2 + c

    def send(src, dst, ssem, rsem, dev):
        return pltpu.make_async_remote_copy(
            src_ref=src, dst_ref=dst, send_sem=ssem, recv_sem=rsem,
            device_id=(dev, 0), device_id_type=pl.DeviceIdType.MESH,
        )

    barrier = pltpu.get_barrier_semaphore()

    def greet(dev):
        pl.semaphore_signal(
            barrier, inc=1, device_id=(dev, 0), device_id_type=pl.DeviceIdType.MESH
        )

    loads = [
        pltpu.make_async_copy(src, dst, w_sem.at[i])
        for i, (src, dst) in enumerate(
            [(sup_hbm, sup), (sdown_hbm, sdown), (up_hbm.at[0], up), (down_hbm.at[0], down)]
        )
    ]
    loads[0].start()
    loads[1].start()
    loads[2].start()
    loads[3].start()
    for dev in (sib, n1, n2):
        greet(dev)

    @pl.when(z > 0)
    def _():
        greet(below)

    @pl.when(z < lines - 1)
    def _():
        greet(above)

    slot_count = chips * 2
    replicas = slot_count // 8
    spans = len_ref.shape[1]
    span = rows // spans
    row_at = lax.broadcasted_iota(jnp.int32, (rows, spans), 0)
    start_at = lax.broadcasted_iota(jnp.int32, (rows, spans), 1) * span
    lane_at = lax.broadcasted_iota(jnp.int32, (rows, EXTRA), 1).astype(F32)
    square = (rows, rows)
    diagonal = lax.broadcasted_iota(jnp.int32, square, 0) == lax.broadcasted_iota(
        jnp.int32, square, 1
    )
    for s in range(steps):
        lens = jnp.minimum(len_ref[pl.ds(s, 1), :], span)
        inside = (row_at >= start_at) & (row_at < start_at + lens)
        alive = jnp.sum(jnp.where(inside, 1.0, 0.0), axis=1, keepdims=True)
        ids = ids_ref[s]
        moved = (ids < replicas) & (second_ref[s] == 1)
        slot = jnp.where(moved, ids + (slot_count - replicas), ids).astype(F32)
        weights = gain_ref[s]
        dense = jnp.zeros((rows, EXTRA), F32)
        for k in range(ids.shape[0]):
            named = jnp.where(diagonal, slot[k : k + 1, :], 0.0)
            heavy = jnp.where(diagonal, weights[k : k + 1, :], 0.0)
            named = jnp.sum(named, axis=1, keepdims=True)
            heavy = jnp.sum(heavy, axis=1, keepdims=True)
            dense = dense + jnp.where(lane_at == named, heavy, 0.0)
        dense = dense * alive
        high = dense.astype(BF)
        x_ref[0, s, :, :half] = own_ref[s, :, :half]
        x_ref[1, s, :, :half] = own_ref[s, :, half:]
        x_ref[0, s, :, half:] = high
        x_ref[1, s, :, half:] = (dense - high.astype(F32)).astype(BF)
        live_ref[s] = jnp.broadcast_to(alive, (rows, 128))

    pl.semaphore_wait(barrier, 3 + jnp.minimum(z, 1) + jnp.minimum(lines - 1 - z, 1))

    def swap(s):
        return send(
            x_ref.at[1 - c, s], gat.at[1 - c, s, chip, c], swap_s.at[s], swap_r.at[s], sib
        )

    def block(s, who):
        return gat.at[c, s, who]

    def go_up(s, zz):
        b = block(s, chip_of(zz, d1, d2))
        return send(b, b, zu_s.at[s, zz], ag_r.at[s, chip_of(zz, d1, d2)], above)

    def go_dn(s, zz):
        b = block(s, chip_of(zz, d1, d2))
        return send(b, b, zd_s.at[s, zz], ag_r.at[s, chip_of(zz, d1, d2)], below)

    def go_d1(s, zz):
        b = block(s, chip_of(zz, d1, d2))
        return send(b, b, d1_s.at[s, zz], ag_r.at[s, chip_of(zz, d1, d2)], n1)

    def go_d2(s, a, zz):
        b = block(s, chip_of(zz, a, d2))
        return send(b, b, d2_s.at[s, a * lines + zz], ag_r.at[s, chip_of(zz, a, d2)], n2)

    def go_sib(s, who):
        b = block(s, who)
        return send(b, b, sib_s.at[s, who], sib_r.at[s, who], sib)

    def arrived(s, who):
        b = block(s, who)
        send(b, b, sib_s.at[s, who], ag_r.at[s, who], sib).wait_recv()

    def spread(s, zz):
        go_d1(s, zz).start()

        @pl.when(zz // 2 == upper)
        def _():
            go_d2(s, d1, zz).start()

        go_sib(s, chip_of(zz, d1, d2)).start()

    def ag_own(s):
        swap(s).wait_recv()

        @pl.when(z < lines - 1)
        def _():
            go_up(s, z).start()

        @pl.when(z > 0)
        def _():
            go_dn(s, z).start()

        spread(s, z)

    def ag_line(s):
        for d in range(1, lines):
            @pl.when(z - d >= 0)
            def _():
                arrived(s, chip_of(z - d, d1, d2))

                @pl.when(z < lines - 1)
                def _():
                    go_up(s, z - d).start()

                spread(s, z - d)

            @pl.when(z + d < lines)
            def _():
                arrived(s, chip_of(z + d, d1, d2))

                @pl.when(z > 0)
                def _():
                    go_dn(s, z + d).start()

                spread(s, z + d)

    def ag_d1(s, k):
        zz = order(k)
        arrived(s, chip_of(zz, 1 - d1, d2))
        go_d2(s, 1 - d1, zz).start()
        go_sib(s, chip_of(zz, 1 - d1, d2)).start()

    def go_z(s, zz, dev):
        who = chip_of(zz, d1, 1 - d2)
        b = block(s, who)
        return send(b, b, cx_s.at[s, zz], ag_r.at[s, who], dev)

    def ag_d2(s, m):
        first_two = 1 - jnp.minimum(m // 2, 1)
        last_two = m // 6
        between = 1 - first_two - last_two
        zz = first_two * same(m) + between * order(m - 2) + last_two * other(m - 6)
        who = chip_of(zz, d1 + between * (1 - 2 * d1), 1 - d2)
        arrived(s, who)

        @pl.when(inner & (m < 2))
        def _():
            go_z(s, zz, toward).start()

        @pl.when(inner & (m >= 6))
        def _():
            go_z(s, zz, away).start()

        go_sib(s, who).start()

    def loop(n, body):
        def step(i, carry):
            body(i)
            return carry

        lax.fori_loop(0, n, step, 0)

    def ag_finish(s):
        def one(who):
            b = gat.at[1 - c, s, who]
            send(b, b, sib_s.at[s, who], sib_r.at[s, who], sib).wait_recv()

        loop(chips, one)

    def cut(i, n):
        return pl.ds(pl.multiple_of(i * n, n), n)

    def shared_up_chunk(i):
        cols = cut(i, 256)
        v = mm(x_ref[0, :, :, :half].reshape(steps * rows, half), sup[:half, cols])
        v = v + mm(x_ref[1, :, :, :half].reshape(steps * rows, half), sup[half:, cols])
        shid[:, cols] = silu(v).astype(BF)

    def shared_down_chunk(j):
        cols = cut(j, 512)
        shout[:, cols] = mm(shid[...], sdown[:, cols])

    def gains(s):
        lane = lax.broadcasted_iota(jnp.int32, (chips * 2 * rows, EXTRA), 1)
        both = gat[0, s, :, :, :, half:].astype(F32) + gat[1, s, :, :, :, half:].astype(F32)
        both = both.reshape(chips * 2 * rows, EXTRA)
        mine = jnp.sum(jnp.where(lane == me, both, 0.0), axis=1, keepdims=True)
        gain[...] = mine.reshape(chips, 2 * rows, 1)

    def up_chunk(s, i):
        cols = cut(i, 256)
        v = mm(gat[0, s, :, :, :, :half].reshape(chips * 2 * rows, half), up[:half, cols])
        v = v + mm(gat[1, s, :, :, :, :half].reshape(chips * 2 * rows, half), up[half:, cols])
        hid[:, :, cols] = silu(v).astype(BF).reshape(chips, 2 * rows, 256)

    def members(t, far):
        there = y + t * (x - y)
        b = (1 - there) if far else there
        return [
            zz * 4 + a * (1 + t) + b * (2 - t) for zz in range(lines) for a in range(2)
        ]

    def down_chunk(s, t, far, j):
        group = members(t, far)
        source = jnp.concatenate([hid[who] for who in group], axis=0)
        scale = jnp.concatenate([gain[who] for who in group], axis=0)
        v = mm(source, down[:, pl.ds(pl.multiple_of(t * half + j * 256, 256), 256)])
        v = (v * scale).astype(BF).reshape(len(group), 2, rows, 256)
        for i, who in enumerate(group):
            part[t, s, who, :, :, cut(j, 256)] = v[i]

    def x0(s, who):
        return send(
            part.at[1 - c, s, who], swapped.at[s, who], x0_s.at[s, who], x0_r.at[s, who], sib
        )

    def x0_start(s, far):
        for who in members(1 - c, far):
            x0(s, who).start()

    def both_cores(s, who):
        x0(s, who).wait_recv()
        return part[c, s, who].astype(F32) + swapped[s, who].astype(F32)

    def f_copy(s, a, zz):
        who = chip_of(zz, a, 1 - d2)
        i = a * lines + zz
        return send(part.at[c, s, who], from_f.at[s, i], f_s.at[s, i], f_r.at[s, i], n2)

    def c_copy(s, zz):
        who = chip_of(zz, d1, 1 - d2)
        return send(part.at[c, s, who], from_c.at[s, zz], c_s.at[s, zz], c_r.at[s, zz], toward)

    def with_c(s, zz):
        c_copy(s, zz).wait_recv()
        return both_cores(s, chip_of(zz, d1, 1 - d2)) + from_c[s, zz].astype(F32)

    def rs_f(s):
        @pl.when(jnp.logical_not(inner))
        def _():
            for k in range(2):
                zz = other(k)
                who = chip_of(zz, d1, 1 - d2)
                part[c, s, who] = both_cores(s, who).astype(BF)
                c_copy(s, zz).start()

        def one(q):
            zz = order(q)
            who = chip_of(zz, 1 - d1, 1 - d2)
            part[c, s, who] = both_cores(s, who).astype(BF)
            f_copy(s, 1 - d1, zz).start()

        loop(lines, one)

    def rs_cross(s):
        @pl.when(inner)
        def _():
            for k in range(2):
                zz = other(k)
                part[c, s, chip_of(zz, d1, 1 - d2)] = with_c(s, zz).astype(BF)
                c_copy(s, zz).start()

    def rs_f_same(s):
        for k in range(2):
            zz = same(k)
            who = chip_of(zz, d1, 1 - d2)

            @pl.when(inner)
            def _():
                part[c, s, who] = with_c(s, zz).astype(BF)

            @pl.when(jnp.logical_not(inner))
            def _():
                part[c, s, who] = both_cores(s, who).astype(BF)

            f_copy(s, d1, zz).start()

    def with_f(s, a, zz):
        f_copy(s, a, zz).wait_recv()
        who = chip_of(zz, a, d2)
        return both_cores(s, who) + from_f[s, a * lines + zz].astype(F32)

    def s_copy(s, zz):
        who = chip_of(zz, 1 - d1, d2)
        return send(part.at[c, s, who], from_s.at[s, zz], s_s.at[s, zz], s_r.at[s, zz], n1)

    def rs_s(s, k):
        zz = order(k)
        who = chip_of(zz, 1 - d1, d2)
        part[c, s, who] = with_f(s, 1 - d1, zz).astype(BF)
        s_copy(s, zz).start()

    def up_copy(s, zz):
        who = chip_of(zz, d1, d2)
        return send(part.at[c, s, who], from_up.at[s, zz], ru_s.at[s, zz], ru_r.at[s, zz], above)

    def dn_copy(s, zz):
        who = chip_of(zz, d1, d2)
        return send(part.at[c, s, who], from_dn.at[s, zz], rd_s.at[s, zz], rd_r.at[s, zz], below)

    def rs_z(s):
        for k in range(lines):
            near = k < 2
            zz = same(k) if near else other(k - 2)
            who = chip_of(zz, d1, d2)
            v = with_f(s, d1, zz) if near else both_cores(s, who)
            s_copy(s, zz).wait_recv()
            part[c, s, who] = (v + from_s[s, zz].astype(F32)).astype(BF)

        for d in range(lines - 1, 0, -1):
            @pl.when(z + d < lines)
            def _():
                zz = z + d
                who = chip_of(zz, d1, d2)

                @pl.when(z > 0)
                def _():
                    up_copy(s, zz).wait_recv()
                    v = part[c, s, who].astype(F32) + from_up[s, zz].astype(F32)
                    part[c, s, who] = v.astype(BF)

                up_copy(s, zz).start()

            @pl.when(z - d >= 0)
            def _():
                zz = z - d
                who = chip_of(zz, d1, d2)

                @pl.when(z < lines - 1)
                def _():
                    dn_copy(s, zz).wait_recv()
                    v = part[c, s, who].astype(F32) + from_dn[s, zz].astype(F32)
                    part[c, s, who] = v.astype(BF)

                dn_copy(s, zz).start()

    def fin(s):
        return send(part.at[c, s, chip, 1 - c], from_fin.at[s], fin_s.at[s], fin_r.at[s], sib)

    def rs_own(s):
        @pl.when(z > 0)
        def _():
            up_copy(s, z).wait_recv()
            v = part[c, s, chip].astype(F32) + from_up[s, z].astype(F32)
            part[c, s, chip] = v.astype(BF)

        @pl.when(z < lines - 1)
        def _():
            dn_copy(s, z).wait_recv()
            v = part[c, s, chip].astype(F32) + from_dn[s, z].astype(F32)
            part[c, s, chip] = v.astype(BF)

        fin(s).start()

    def write(s):
        fin(s).wait_recv()
        keep = part[c, s, chip, c].astype(F32)
        other = from_fin[s].astype(F32)
        lead = jnp.where(c == 0, keep, other)
        tail = jnp.where(c == 0, other, keep)
        alive = live_ref[s, :, :1]
        mine = pl.ds(s * rows, rows)
        out_ref[s, :, :half] = ((lead + shout[mine, :half]) * alive).astype(out_ref.dtype)
        out_ref[s, :, half:] = ((tail + shout[mine, half:]) * alive).astype(out_ref.dtype)

    for s in range(steps):
        gat[c, s, chip, c] = x_ref[c, s]
        swap(s).start()
    ag_own(0)
    ag_line(0)
    loads[0].wait()

    def first(k):
        ag_d1(0, k)
        shared_up_chunk(k)

    loop(lines, first)
    ag_own(1)
    ag_line(1)
    loads[1].wait()

    def second(m):
        ag_d2(0, m)
        shared_down_chunk(m)

    loop(2 * lines - 1, second)
    ag_d2(0, 2 * lines - 1)
    ag_finish(0)
    loads[2].wait()
    gains(0)

    def third(i):
        up_chunk(0, i)
        ag_d1(1, i)

    loop(hidden_units // 256, third)
    loads[3].wait()
    chunks = half // 256
    late = chunks - lines
    loop(chunks, lambda j: down_chunk(0, 1 - c, True, j))
    x0_start(0, True)
    loop(chunks, lambda j: down_chunk(0, c, True, j))
    rs_f(0)

    def fourth(j):
        down_chunk(0, 1 - c, False, j)

        @pl.when(j >= late)
        def _():
            ag_d2(1, j - late)

    loop(chunks, fourth)
    x0_start(0, False)
    rs_cross(0)

    def fifth(j):
        down_chunk(0, c, False, j)

        @pl.when(j >= late)
        def _():
            ag_d2(1, j - late + lines)

    loop(chunks, fifth)
    rs_f_same(0)
    ag_finish(1)
    gains(1)
    loop(hidden_units // 256, lambda i: up_chunk(1, i))

    def sixth(j):
        down_chunk(1, 1 - c, True, j)

        @pl.when(j >= late)
        def _():
            rs_s(0, j - late)

    loop(chunks, sixth)
    x0_start(1, True)
    loop(chunks, lambda j: down_chunk(1, c, True, j))
    rs_f(1)
    loop(chunks, lambda j: down_chunk(1, 1 - c, False, j))
    x0_start(1, False)
    rs_cross(1)
    loop(chunks, lambda j: down_chunk(1, c, False, j))
    rs_f_same(1)
    rs_z(0)
    loop(lines, lambda k: rs_s(1, k))
    rs_own(0)
    rs_z(1)
    write(0)
    rs_own(1)
    write(1)

    for s in range(steps):
        swap(s).wait_send()
        fin(s).wait_send()

        def planes(zz):
            go_d1(s, zz).wait_send()
            go_d2(s, 1 - d1, zz).wait_send()
            f_copy(s, 1 - d1, zz).wait_send()

            @pl.when(zz // 2 == upper)
            def _():
                go_d2(s, d1, zz).wait_send()
                f_copy(s, d1, zz).wait_send()

            @pl.when(inner)
            def _():
                go_z(s, zz, toward).wait_send()

            @pl.when(zz // 2 != upper)
            def _():
                c_copy(s, zz).wait_send()

            s_copy(s, zz).wait_send()

            @pl.when((zz <= z) & (z < lines - 1))
            def _():
                go_up(s, zz).wait_send()

            @pl.when((zz >= z) & (z > 0))
            def _():
                go_dn(s, zz).wait_send()

            @pl.when(zz > z)
            def _():
                up_copy(s, zz).wait_send()

            @pl.when(zz < z)
            def _():
                dn_copy(s, zz).wait_send()

        loop(lines, planes)

        def siblings(who):
            go_sib(s, who).wait_send()
            x0(s, who).wait_send()

        loop(chips, siblings)


def fused_layer(
    hidden_rows, draft_len, expert_ids, replica, route_gain, slot_up, slot_down, shared_up, shared_down
):
    slot_count = lax.axis_size("expert")
    steps, rows, width = hidden_rows.shape
    half = width // 2
    chips = slot_count // 2
    lines = chips // 4
    hidden_units = slot_up.shape[2]
    vm = pl.BlockSpec(memory_space=pltpu.VMEM)
    hbm = pl.BlockSpec(memory_space=pl.ANY)
    dma = pltpu.SemaphoreType.DMA
    flops = 4 * steps * rows * (slot_count + 1) * width * hidden_units
    return pl.pallas_call(
        fused,
        out_shape=jax.ShapeDtypeStruct((steps, rows, width), BF),
        in_specs=[vm] * 5 + [hbm] * 4,
        out_specs=vm,
        scratch_shapes=[
            pltpu.VMEM((2, steps, rows, half + EXTRA), BF),
            pltpu.VMEM((steps, rows, 128), F32),
            pltpu.VMEM((2, steps, chips, 2, rows, half + EXTRA), BF),
            pltpu.VMEM((2, steps, chips, 2, rows, half), BF),
            pltpu.VMEM((steps, chips, 2, rows, half), BF),
            pltpu.VMEM((steps, 2 * lines, 2, rows, half), BF),
            pltpu.VMEM((steps, lines, 2, rows, half), BF),
            pltpu.VMEM((steps, lines, 2, rows, half), BF),
            pltpu.VMEM((steps, lines, 2, rows, half), BF),
            pltpu.VMEM((steps, lines, 2, rows, half), BF),
            pltpu.VMEM((steps, rows, half), BF),
            pltpu.VMEM(slot_up.shape[1:], BF),
            pltpu.VMEM(slot_down.shape[1:], BF),
            pltpu.VMEM(shared_up.shape, BF),
            pltpu.VMEM(shared_down.shape, BF),
            pltpu.VMEM((chips, 2 * rows, hidden_units), BF),
            pltpu.VMEM((chips, 2 * rows, 1), F32),
            pltpu.VMEM((steps * rows, shared_up.shape[1]), BF),
            pltpu.VMEM((steps * rows, width), F32),
            dma((4,)), dma((steps,)), dma((steps,)),
            dma((steps, lines)), dma((steps, lines)), dma((steps, lines)),
            dma((steps, 2 * lines)), dma((steps, chips)),
            dma((steps, chips)), dma((steps, chips)),
            dma((steps, chips)), dma((steps, chips)),
            dma((steps, 2 * lines)), dma((steps, 2 * lines)),
            dma((steps, lines)), dma((steps, lines)),
            dma((steps, lines)), dma((steps, lines)),
            dma((steps, lines)), dma((steps, lines)),
            dma((steps,)), dma((steps,)),
            dma((steps, lines)), dma((steps, lines)), dma((steps, lines)),
        ],
        compiler_params=pltpu.CompilerParams(
            collective_id=0, has_side_effects=True, vmem_limit_bytes=62 * 1024 * 1024
        ),
        cost_estimate=pl.CostEstimate(
            flops=flops, bytes_accessed=4 * 2 * width * hidden_units, transcendentals=0
        ),
        name="fused_layer",
    )(
        hidden_rows, draft_len, jnp.swapaxes(expert_ids, 1, 2), jnp.swapaxes(replica, 1, 2),
        jnp.swapaxes(route_gain, 1, 2), slot_up, slot_down, shared_up, shared_down,
    )


def slot_gains(lengths, chosen, second, gains, slot_count):
    row_count = chosen.shape[1]
    span = row_count // lengths.shape[1]
    replicas = slot_count // 8
    experts_all = slot_count - replicas
    limit = jnp.repeat(lengths, span, axis=1, total_repeat_length=row_count)
    live = (jnp.arange(row_count, dtype=jnp.int32)[None] % span < limit).astype(jnp.float32)
    slot = jnp.where((chosen < replicas) & (second == 1), chosen + experts_all, chosen)
    hit = slot[..., None] == jnp.arange(slot_count, dtype=jnp.int32)
    dense = jnp.sum(jnp.where(hit, gains[..., None], 0.0), axis=2)
    return live, dense * live[..., None]


def shards(
    hidden_rows,
    draft_len,
    expert_ids,
    replica,
    route_gain,
    slot_up,
    slot_down,
    shared_up,
    shared_down,
):
    slot_count = lax.axis_size("expert")
    me = lax.axis_index("expert")
    steps, rows, _ = hidden_rows.shape
    own = lax.all_gather(hidden_rows, "tensor", axis=2, tiled=True)
    width = own.shape[2]
    live, dense = slot_gains(draft_len, expert_ids, replica, route_gain, slot_count)
    high = dense.astype(jnp.bfloat16)
    low = (dense - high.astype(jnp.float32)).astype(jnp.bfloat16)
    packed = jnp.concatenate([own, high, low], axis=2)
    routed = []
    for index in range(steps):
        everything = lax.all_gather(packed[index], "expert", axis=0, tiled=True)
        source = everything[:, :width]
        pick = jnp.arange(slot_count) == me
        both = everything[:, width:].astype(jnp.float32)
        both = both[:, :slot_count] + both[:, slot_count:]
        weight = jnp.sum(jnp.where(pick[None], both, 0.0), axis=1, keepdims=True)
        hidden = jax.nn.silu(
            jnp.dot(source, slot_up[0], preferred_element_type=jnp.float32)
        ).astype(jnp.bfloat16)
        part = jnp.dot(hidden, slot_down[0], preferred_element_type=jnp.float32)
        part = (part * weight).astype(jnp.bfloat16)
        part = lax.psum_scatter(part, "tensor", scatter_dimension=1, tiled=True)
        routed.append(lax.psum_scatter(part, "expert", scatter_dimension=0, tiled=True))
    flat = own.reshape(steps * rows, width)
    shared_act = jax.nn.silu(
        jnp.dot(flat, shared_up, preferred_element_type=jnp.float32)
    ).astype(jnp.bfloat16)
    shared_out = jnp.dot(shared_act, shared_down, preferred_element_type=jnp.float32)
    if lax.axis_size("tensor") > 1:
        shared_out = lax.psum_scatter(shared_out, "tensor", scatter_dimension=1, tiled=True)
    shared_out = shared_out.reshape(steps, rows, -1)
    total = jnp.stack(routed).astype(jnp.float32) + shared_out
    return (total * live[..., None]).astype(jnp.bfloat16)


def solution(mesh):
    fits = mesh.shape["tensor"] == 1 and mesh.shape["expert"] == 32
    return jax.shard_map(
        fused_layer if fits else shards,
        mesh=mesh,
        in_specs=(
            P(None, "expert", "tensor"),
            P(None, "expert"),
            P(None, "expert", None),
            P(None, "expert", None),
            P(None, "expert", None),
            P("expert", None, "tensor"),
            P("expert", "tensor", None),
            P(None, "tensor"),
            P("tensor", None),
        ),
        out_specs=P(None, "expert", "tensor"),
        check_vma=False,
    )
```

```python
import functools
import jax
import jax.numpy as jnp
from jax import lax
from jax.experimental import pallas as pl
from jax.experimental.pallas import tpu as pltpu
from jax.sharding import PartitionSpec as P

BF = jnp.bfloat16
F32 = jnp.float32
EXTRA = 128


def mm(a, b):
    return jnp.dot(a, b, preferred_element_type=F32)


def silu(v):
    return v / (1.0 + jnp.exp(-v))


def fused(
    own_ref, len_ref, ids_ref, second_ref, gain_ref, up_hbm, down_hbm, sup_hbm, sdown_hbm,
    out_ref, x_ref, live_ref, gat, part, swapped, from_f, from_s, from_up, from_dn, from_fin,
    up, down, sup, sdown, hid, gain, shid, shout,
    w_sem, swap_s, swap_r, zu_s, zd_s, d1_s, d2_s, ag_r, sib_s, sib_r,
    x0_s, x0_r, f_s, f_r, s_s, s_r, ru_s, ru_r, rd_s, rd_r, fin_s, fin_r,
):
    steps = gat.shape[1]
    chips = gat.shape[2]
    rows = gat.shape[4]
    half = part.shape[5]
    lines = chips // 4
    hidden_units = up.shape[1]
    me = lax.axis_index("expert")
    c = me % 2
    chip = me // 2
    x = chip % 2
    y = (chip // 2) % 2
    z = chip // 4
    d1 = x + c * (y - x)
    d2 = y + c * (x - y)
    w1 = 1 + c
    w2 = 2 - c
    turn = 1 - 2 * (z // (lines // 2))

    def chip_of(zz, a, b):
        return zz * 4 + a * w1 + b * w2

    def order(k):
        return (z + turn * k + lines) % lines

    sib = chip * 2 + (1 - c)
    above = me + 8
    below = me - 8
    n1 = chip_of(z, 1 - d1, d2) * 2 + c
    n2 = chip_of(z, d1, 1 - d2) * 2 + c

    def send(src, dst, ssem, rsem, dev):
        return pltpu.make_async_remote_copy(
            src_ref=src, dst_ref=dst, send_sem=ssem, recv_sem=rsem,
            device_id=(dev, 0), device_id_type=pl.DeviceIdType.MESH,
        )

    barrier = pltpu.get_barrier_semaphore()

    def greet(dev):
        pl.semaphore_signal(
            barrier, inc=1, device_id=(dev, 0), device_id_type=pl.DeviceIdType.MESH
        )

    loads = [
        pltpu.make_async_copy(src, dst, w_sem.at[i])
        for i, (src, dst) in enumerate(
            [(sup_hbm, sup), (sdown_hbm, sdown), (up_hbm.at[0], up), (down_hbm.at[0], down)]
        )
    ]
    loads[0].start()
    loads[1].start()
    loads[2].start()
    loads[3].start()
    for dev in (sib, n1, n2):
        greet(dev)

    @pl.when(z > 0)
    def _():
        greet(below)

    @pl.when(z < lines - 1)
    def _():
        greet(above)

    slot_count = chips * 2
    replicas = slot_count // 8
    spans = len_ref.shape[1]
    span = rows // spans
    row_at = lax.broadcasted_iota(jnp.int32, (rows, spans), 0)
    start_at = lax.broadcasted_iota(jnp.int32, (rows, spans), 1) * span
    lane_at = lax.broadcasted_iota(jnp.int32, (rows, EXTRA), 1).astype(F32)
    square = (rows, rows)
    diagonal = lax.broadcasted_iota(jnp.int32, square, 0) == lax.broadcasted_iota(
        jnp.int32, square, 1
    )
    for s in range(steps):
        lens = jnp.minimum(len_ref[pl.ds(s, 1), :], span)
        inside = (row_at >= start_at) & (row_at < start_at + lens)
        alive = jnp.sum(jnp.where(inside, 1.0, 0.0), axis=1, keepdims=True)
        ids = ids_ref[s]
        moved = (ids < replicas) & (second_ref[s] == 1)
        slot = jnp.where(moved, ids + (slot_count - replicas), ids).astype(F32)
        weights = gain_ref[s]
        dense = jnp.zeros((rows, EXTRA), F32)
        for k in range(ids.shape[0]):
            named = jnp.where(diagonal, slot[k : k + 1, :], 0.0)
            heavy = jnp.where(diagonal, weights[k : k + 1, :], 0.0)
            named = jnp.sum(named, axis=1, keepdims=True)
            heavy = jnp.sum(heavy, axis=1, keepdims=True)
            dense = dense + jnp.where(lane_at == named, heavy, 0.0)
        dense = dense * alive
        high = dense.astype(BF)
        x_ref[0, s, :, :half] = own_ref[s, :, :half]
        x_ref[1, s, :, :half] = own_ref[s, :, half:]
        x_ref[0, s, :, half:] = high
        x_ref[1, s, :, half:] = (dense - high.astype(F32)).astype(BF)
        live_ref[s] = jnp.broadcast_to(alive, (rows, 128))

    pl.semaphore_wait(barrier, 3 + jnp.minimum(z, 1) + jnp.minimum(lines - 1 - z, 1))

    def swap(s):
        return send(
            x_ref.at[1 - c, s], gat.at[1 - c, s, chip, c], swap_s.at[s], swap_r.at[s], sib
        )

    def block(s, who):
        return gat.at[c, s, who]

    def go_up(s, zz):
        b = block(s, chip_of(zz, d1, d2))
        return send(b, b, zu_s.at[s, zz], ag_r.at[s, chip_of(zz, d1, d2)], above)

    def go_dn(s, zz):
        b = block(s, chip_of(zz, d1, d2))
        return send(b, b, zd_s.at[s, zz], ag_r.at[s, chip_of(zz, d1, d2)], below)

    def go_d1(s, zz):
        b = block(s, chip_of(zz, d1, d2))
        return send(b, b, d1_s.at[s, zz], ag_r.at[s, chip_of(zz, d1, d2)], n1)

    def go_d2(s, a, zz):
        b = block(s, chip_of(zz, a, d2))
        return send(b, b, d2_s.at[s, a * lines + zz], ag_r.at[s, chip_of(zz, a, d2)], n2)

    def go_sib(s, who):
        b = block(s, who)
        return send(b, b, sib_s.at[s, who], sib_r.at[s, who], sib)

    def arrived(s, who):
        b = block(s, who)
        send(b, b, sib_s.at[s, who], ag_r.at[s, who], sib).wait_recv()

    def spread(s, zz):
        go_d1(s, zz).start()
        go_d2(s, d1, zz).start()
        go_sib(s, chip_of(zz, d1, d2)).start()

    def ag_own(s):
        swap(s).wait_recv()

        @pl.when(z < lines - 1)
        def _():
            go_up(s, z).start()

        @pl.when(z > 0)
        def _():
            go_dn(s, z).start()

    def ag_line(s, d):
        @pl.when(z - d >= 0)
        def _():
            arrived(s, chip_of(z - d, d1, d2))

            @pl.when(z < lines - 1)
            def _():
                go_up(s, z - d).start()

            if s == 0:
                spread(s, z - d)

        @pl.when(z + d < lines)
        def _():
            arrived(s, chip_of(z + d, d1, d2))

            @pl.when(z > 0)
            def _():
                go_dn(s, z + d).start()

            if s == 0:
                spread(s, z + d)

    def ag_d1(s, k):
        zz = order(k)
        arrived(s, chip_of(zz, 1 - d1, d2))
        go_d2(s, 1 - d1, zz).start()
        go_sib(s, chip_of(zz, 1 - d1, d2)).start()

    def ag_d2(s, m):
        a = (d1 + m // lines) % 2
        who = chip_of(order(m % lines), a, 1 - d2)
        arrived(s, who)
        go_sib(s, who).start()

    def loop(n, body):
        def step(i, carry):
            body(i)
            return carry

        lax.fori_loop(0, n, step, 0)

    def ag_finish(s):
        def one(who):
            b = gat.at[1 - c, s, who]
            send(b, b, sib_s.at[s, who], sib_r.at[s, who], sib).wait_recv()

        loop(chips, one)

    def cut(i, n):
        return pl.ds(pl.multiple_of(i * n, n), n)

    def shared_up_chunk(i):
        cols = cut(i, 256)
        v = mm(x_ref[0, :, :, :half].reshape(steps * rows, half), sup[:half, cols])
        v = v + mm(x_ref[1, :, :, :half].reshape(steps * rows, half), sup[half:, cols])
        shid[:, cols] = silu(v).astype(BF)

    def shared_down_chunk(j):
        cols = cut(j, 512)
        shout[:, cols] = mm(shid[...], sdown[:, cols])

    def gains(s):
        lane = lax.broadcasted_iota(jnp.int32, (chips * 2 * rows, EXTRA), 1)
        both = gat[0, s, :, :, :, half:].astype(F32) + gat[1, s, :, :, :, half:].astype(F32)
        both = both.reshape(chips * 2 * rows, EXTRA)
        mine = jnp.sum(jnp.where(lane == me, both, 0.0), axis=1, keepdims=True)
        gain[...] = mine.reshape(chips, 2 * rows, 1)

    def up_chunk(s, i):
        cols = cut(i, 256)
        v = mm(gat[0, s, :, :, :, :half].reshape(chips * 2 * rows, half), up[:half, cols])
        v = v + mm(gat[1, s, :, :, :, :half].reshape(chips * 2 * rows, half), up[half:, cols])
        hid[:, :, cols] = silu(v).astype(BF).reshape(chips, 2 * rows, 256)

    def members(t, far):
        there = y + t * (x - y)
        b = (1 - there) if far else there
        return [
            zz * 4 + a * (1 + t) + b * (2 - t) for zz in range(lines) for a in range(2)
        ]

    def down_chunk(s, t, far, j):
        group = members(t, far)
        source = jnp.concatenate([hid[who] for who in group], axis=0)
        scale = jnp.concatenate([gain[who] for who in group], axis=0)
        v = mm(source, down[:, pl.ds(pl.multiple_of(t * half + j * 256, 256), 256)])
        v = (v * scale).astype(BF).reshape(len(group), 2, rows, 256)
        for i, who in enumerate(group):
            part[t, s, who, :, :, cut(j, 256)] = v[i]

    def x0(s, who):
        return send(
            part.at[1 - c, s, who], swapped.at[s, who], x0_s.at[s, who], x0_r.at[s, who], sib
        )

    def x0_start(s, far):
        for who in members(1 - c, far):
            x0(s, who).start()

    def both_cores(s, who):
        x0(s, who).wait_recv()
        return part[c, s, who].astype(F32) + swapped[s, who].astype(F32)

    def f_copy(s, a, zz):
        who = chip_of(zz, a, 1 - d2)
        i = a * lines + zz
        return send(part.at[c, s, who], from_f.at[s, i], f_s.at[s, i], f_r.at[s, i], n2)

    def rs_f(s, q):
        a = (1 - d1 + q // lines) % 2
        zz = order(q % lines)
        who = chip_of(zz, a, 1 - d2)
        part[c, s, who] = both_cores(s, who).astype(BF)
        f_copy(s, a, zz).start()

    def with_f(s, a, zz):
        f_copy(s, a, zz).wait_recv()
        who = chip_of(zz, a, d2)
        return both_cores(s, who) + from_f[s, a * lines + zz].astype(F32)

    def s_copy(s, zz):
        who = chip_of(zz, 1 - d1, d2)
        return send(part.at[c, s, who], from_s.at[s, zz], s_s.at[s, zz], s_r.at[s, zz], n1)

    def rs_s(s, k):
        zz = order(k)
        who = chip_of(zz, 1 - d1, d2)
        part[c, s, who] = with_f(s, 1 - d1, zz).astype(BF)
        s_copy(s, zz).start()

    def up_copy(s, zz):
        who = chip_of(zz, d1, d2)
        return send(part.at[c, s, who], from_up.at[s, zz], ru_s.at[s, zz], ru_r.at[s, zz], above)

    def dn_copy(s, zz):
        who = chip_of(zz, d1, d2)
        return send(part.at[c, s, who], from_dn.at[s, zz], rd_s.at[s, zz], rd_r.at[s, zz], below)

    def rs_collect(s):
        def collect(k):
            zz = order(k)
            who = chip_of(zz, d1, d2)
            v = with_f(s, d1, zz)
            s_copy(s, zz).wait_recv()
            part[c, s, who] = (v + from_s[s, zz].astype(F32)).astype(BF)

        loop(lines, collect)

    def rs_hop(s, d):
        @pl.when(z + d < lines)
        def _():
            zz = z + d
            who = chip_of(zz, d1, d2)

            @pl.when(z > 0)
            def _():
                up_copy(s, zz).wait_recv()
                v = part[c, s, who].astype(F32) + from_up[s, zz].astype(F32)
                part[c, s, who] = v.astype(BF)

            up_copy(s, zz).start()

        @pl.when(z - d >= 0)
        def _():
            zz = z - d
            who = chip_of(zz, d1, d2)

            @pl.when(z < lines - 1)
            def _():
                dn_copy(s, zz).wait_recv()
                v = part[c, s, who].astype(F32) + from_dn[s, zz].astype(F32)
                part[c, s, who] = v.astype(BF)

            dn_copy(s, zz).start()

    def fin(s):
        return send(part.at[c, s, chip, 1 - c], from_fin.at[s], fin_s.at[s], fin_r.at[s], sib)

    def rs_own(s):
        @pl.when(z > 0)
        def _():
            up_copy(s, z).wait_recv()
            v = part[c, s, chip].astype(F32) + from_up[s, z].astype(F32)
            part[c, s, chip] = v.astype(BF)

        @pl.when(z < lines - 1)
        def _():
            dn_copy(s, z).wait_recv()
            v = part[c, s, chip].astype(F32) + from_dn[s, z].astype(F32)
            part[c, s, chip] = v.astype(BF)

        fin(s).start()

    def write(s):
        fin(s).wait_recv()
        keep = part[c, s, chip, c].astype(F32)
        other = from_fin[s].astype(F32)
        lead = jnp.where(c == 0, keep, other)
        tail = jnp.where(c == 0, other, keep)
        alive = live_ref[s, :, :1]
        mine = pl.ds(s * rows, rows)
        out_ref[s, :, :half] = ((lead + shout[mine, :half]) * alive).astype(out_ref.dtype)
        out_ref[s, :, half:] = ((tail + shout[mine, half:]) * alive).astype(out_ref.dtype)

    for s in range(steps):
        gat[c, s, chip, c] = x_ref[c, s]
        swap(s).start()
    ag_own(0)
    spread(0, z)
    ag_own(1)
    for d in range(1, lines):
        ag_line(0, d)
        ag_line(1, d)
        if d < lines - 1:
            ag_d1(0, d - 1)
    loads[0].wait()

    def first(k):
        shared_up_chunk(k)

        @pl.when(k < 2)
        def _():
            ag_d1(0, k + lines - 2)

    loop(lines, first)
    loop(lines, lambda k: spread(1, order(k)))
    loads[1].wait()

    def second(m):
        ag_d2(0, m)
        shared_down_chunk(m)

    loop(2 * lines - 1, second)
    ag_d2(0, 2 * lines - 1)
    ag_finish(0)
    loads[2].wait()
    gains(0)

    def third(i):
        up_chunk(0, i)
        ag_d1(1, i)

    loop(hidden_units // 256, third)
    loads[3].wait()
    chunks = half // 256
    late = chunks - lines
    loop(chunks, lambda j: down_chunk(0, 1 - c, True, j))
    x0_start(0, True)
    loop(chunks, lambda j: down_chunk(0, c, True, j))
    loop(2 * lines, lambda q: rs_f(0, q))

    def fourth(j):
        down_chunk(0, 1 - c, False, j)

        @pl.when(j >= late)
        def _():
            ag_d2(1, j - late)

    loop(chunks, fourth)
    x0_start(0, False)

    def fifth(j):
        down_chunk(0, c, False, j)

        @pl.when(j >= late)
        def _():
            ag_d2(1, j - late + lines)

    loop(chunks, fifth)
    ag_finish(1)
    gains(1)
    loop(hidden_units // 256, lambda i: up_chunk(1, i))

    def sixth(j):
        down_chunk(1, 1 - c, True, j)

        @pl.when(j >= late)
        def _():
            rs_s(0, j - late)

    loop(chunks, sixth)
    x0_start(1, True)
    loop(chunks, lambda j: down_chunk(1, c, True, j))
    loop(2 * lines, lambda q: rs_f(1, q))
    rs_collect(0)
    rs_hop(0, 3)
    loop(chunks, lambda j: down_chunk(1, 1 - c, False, j))
    x0_start(1, False)
    rs_hop(0, 2)
    loop(chunks, lambda j: down_chunk(1, c, False, j))
    rs_hop(0, 1)
    loop(lines, lambda k: rs_s(1, k))
    rs_own(0)
    rs_collect(1)
    rs_hop(1, 3)
    rs_hop(1, 2)
    rs_hop(1, 1)
    write(0)
    rs_own(1)
    write(1)

    for s in range(steps):
        swap(s).wait_send()
        fin(s).wait_send()

        def planes(zz):
            go_d1(s, zz).wait_send()
            go_d2(s, 0, zz).wait_send()
            go_d2(s, 1, zz).wait_send()
            f_copy(s, 0, zz).wait_send()
            f_copy(s, 1, zz).wait_send()
            s_copy(s, zz).wait_send()

            @pl.when((zz <= z) & (z < lines - 1))
            def _():
                go_up(s, zz).wait_send()

            @pl.when((zz >= z) & (z > 0))
            def _():
                go_dn(s, zz).wait_send()

            @pl.when(zz > z)
            def _():
                up_copy(s, zz).wait_send()

            @pl.when(zz < z)
            def _():
                dn_copy(s, zz).wait_send()

        loop(lines, planes)

        def siblings(who):
            go_sib(s, who).wait_send()
            x0(s, who).wait_send()

        loop(chips, siblings)


def fused_layer(
    hidden_rows, draft_len, expert_ids, replica, route_gain, slot_up, slot_down, shared_up, shared_down
):
    slot_count = lax.axis_size("expert")
    steps, rows, width = hidden_rows.shape
    half = width // 2
    chips = slot_count // 2
    lines = chips // 4
    hidden_units = slot_up.shape[2]
    vm = pl.BlockSpec(memory_space=pltpu.VMEM)
    hbm = pl.BlockSpec(memory_space=pl.ANY)
    dma = pltpu.SemaphoreType.DMA
    flops = 4 * steps * rows * (slot_count + 1) * width * hidden_units
    return pl.pallas_call(
        fused,
        out_shape=jax.ShapeDtypeStruct((steps, rows, width), BF),
        in_specs=[vm] * 5 + [hbm] * 4,
        out_specs=vm,
        scratch_shapes=[
            pltpu.VMEM((2, steps, rows, half + EXTRA), BF),
            pltpu.VMEM((steps, rows, 128), F32),
            pltpu.VMEM((2, steps, chips, 2, rows, half + EXTRA), BF),
            pltpu.VMEM((2, steps, chips, 2, rows, half), BF),
            pltpu.VMEM((steps, chips, 2, rows, half), BF),
            pltpu.VMEM((steps, 2 * lines, 2, rows, half), BF),
            pltpu.VMEM((steps, lines, 2, rows, half), BF),
            pltpu.VMEM((steps, lines, 2, rows, half), BF),
            pltpu.VMEM((steps, lines, 2, rows, half), BF),
            pltpu.VMEM((steps, rows, half), BF),
            pltpu.VMEM(slot_up.shape[1:], BF),
            pltpu.VMEM(slot_down.shape[1:], BF),
            pltpu.VMEM(shared_up.shape, BF),
            pltpu.VMEM(shared_down.shape, BF),
            pltpu.VMEM((chips, 2 * rows, hidden_units), BF),
            pltpu.VMEM((chips, 2 * rows, 1), F32),
            pltpu.VMEM((steps * rows, shared_up.shape[1]), BF),
            pltpu.VMEM((steps * rows, width), F32),
            dma((4,)), dma((steps,)), dma((steps,)),
            dma((steps, lines)), dma((steps, lines)), dma((steps, lines)),
            dma((steps, 2 * lines)), dma((steps, chips)),
            dma((steps, chips)), dma((steps, chips)),
            dma((steps, chips)), dma((steps, chips)),
            dma((steps, 2 * lines)), dma((steps, 2 * lines)),
            dma((steps, lines)), dma((steps, lines)),
            dma((steps, lines)), dma((steps, lines)),
            dma((steps, lines)), dma((steps, lines)),
            dma((steps,)), dma((steps,)),
        ],
        compiler_params=pltpu.CompilerParams(
            collective_id=0, has_side_effects=True, vmem_limit_bytes=62 * 1024 * 1024
        ),
        cost_estimate=pl.CostEstimate(
            flops=flops, bytes_accessed=4 * 2 * width * hidden_units, transcendentals=0
        ),
        name="fused_layer",
    )(
        hidden_rows, draft_len, jnp.swapaxes(expert_ids, 1, 2), jnp.swapaxes(replica, 1, 2),
        jnp.swapaxes(route_gain, 1, 2), slot_up, slot_down, shared_up, shared_down,
    )


def slot_gains(lengths, chosen, second, gains, slot_count):
    row_count = chosen.shape[1]
    span = row_count // lengths.shape[1]
    replicas = slot_count // 8
    experts_all = slot_count - replicas
    limit = jnp.repeat(lengths, span, axis=1, total_repeat_length=row_count)
    live = (jnp.arange(row_count, dtype=jnp.int32)[None] % span < limit).astype(jnp.float32)
    slot = jnp.where((chosen < replicas) & (second == 1), chosen + experts_all, chosen)
    hit = slot[..., None] == jnp.arange(slot_count, dtype=jnp.int32)
    dense = jnp.sum(jnp.where(hit, gains[..., None], 0.0), axis=2)
    return live, dense * live[..., None]


def shards(
    hidden_rows,
    draft_len,
    expert_ids,
    replica,
    route_gain,
    slot_up,
    slot_down,
    shared_up,
    shared_down,
):
    slot_count = lax.axis_size("expert")
    me = lax.axis_index("expert")
    steps, rows, _ = hidden_rows.shape
    own = lax.all_gather(hidden_rows, "tensor", axis=2, tiled=True)
    width = own.shape[2]
    live, dense = slot_gains(draft_len, expert_ids, replica, route_gain, slot_count)
    high = dense.astype(jnp.bfloat16)
    low = (dense - high.astype(jnp.float32)).astype(jnp.bfloat16)
    packed = jnp.concatenate([own, high, low], axis=2)
    routed = []
    for index in range(steps):
        everything = lax.all_gather(packed[index], "expert", axis=0, tiled=True)
        source = everything[:, :width]
        pick = jnp.arange(slot_count) == me
        both = everything[:, width:].astype(jnp.float32)
        both = both[:, :slot_count] + both[:, slot_count:]
        weight = jnp.sum(jnp.where(pick[None], both, 0.0), axis=1, keepdims=True)
        hidden = jax.nn.silu(
            jnp.dot(source, slot_up[0], preferred_element_type=jnp.float32)
        ).astype(jnp.bfloat16)
        part = jnp.dot(hidden, slot_down[0], preferred_element_type=jnp.float32)
        part = (part * weight).astype(jnp.bfloat16)
        part = lax.psum_scatter(part, "tensor", scatter_dimension=1, tiled=True)
        routed.append(lax.psum_scatter(part, "expert", scatter_dimension=0, tiled=True))
    flat = own.reshape(steps * rows, width)
    shared_act = jax.nn.silu(
        jnp.dot(flat, shared_up, preferred_element_type=jnp.float32)
    ).astype(jnp.bfloat16)
    shared_out = jnp.dot(shared_act, shared_down, preferred_element_type=jnp.float32)
    if lax.axis_size("tensor") > 1:
        shared_out = lax.psum_scatter(shared_out, "tensor", scatter_dimension=1, tiled=True)
    shared_out = shared_out.reshape(steps, rows, -1)
    total = jnp.stack(routed).astype(jnp.float32) + shared_out
    return (total * live[..., None]).astype(jnp.bfloat16)


def solution(mesh):
    fits = mesh.shape["tensor"] == 1 and mesh.shape["expert"] == 32
    return jax.shard_map(
        fused_layer if fits else shards,
        mesh=mesh,
        in_specs=(
            P(None, "expert", "tensor"),
            P(None, "expert"),
            P(None, "expert", None),
            P(None, "expert", None),
            P(None, "expert", None),
            P("expert", None, "tensor"),
            P("expert", "tensor", None),
            P(None, "tensor"),
            P("tensor", None),
        ),
        out_specs=P(None, "expert", "tensor"),
        check_vma=False,
    )
```

```python
import functools
import jax
import jax.numpy as jnp
from jax import lax
from jax.experimental import pallas as pl
from jax.experimental.pallas import tpu as pltpu
from jax.sharding import PartitionSpec as P

BF = jnp.bfloat16
F32 = jnp.float32
EXTRA = 128


def mm(a, b):
    return jnp.dot(a, b, preferred_element_type=F32)


def silu(v):
    return v / (1.0 + jnp.exp(-v))


def fused(
    own_ref, len_ref, ids_ref, second_ref, gain_ref, up_hbm, down_hbm, sup_hbm, sdown_hbm,
    out_ref, x_ref, live_ref, gat, part, swapped, from_f, from_s, from_up, from_dn, from_fin,
    up, down, sup, sdown, hid, gain, shid, shout,
    w_sem, swap_s, swap_r, zu_s, zd_s, d1_s, d2_s, ag_r, sib_s, sib_r,
    x0_s, x0_r, f_s, f_r, s_s, s_r, ru_s, ru_r, rd_s, rd_r, fin_s, fin_r,
):
    steps = gat.shape[1]
    chips = gat.shape[2]
    rows = gat.shape[4]
    half = part.shape[5]
    lines = chips // 4
    hidden_units = up.shape[1]
    me = lax.axis_index("expert")
    c = me % 2
    chip = me // 2
    x = chip % 2
    y = (chip // 2) % 2
    z = chip // 4
    d1 = x + c * (y - x)
    d2 = y + c * (x - y)
    w1 = 1 + c
    w2 = 2 - c
    turn = 1 - 2 * (z // (lines // 2))

    def chip_of(zz, a, b):
        return zz * 4 + a * w1 + b * w2

    def order(k):
        return (z + turn * k + lines) % lines

    sib = chip * 2 + (1 - c)
    above = me + 8
    below = me - 8
    n1 = chip_of(z, 1 - d1, d2) * 2 + c
    n2 = chip_of(z, d1, 1 - d2) * 2 + c

    def send(src, dst, ssem, rsem, dev):
        return pltpu.make_async_remote_copy(
            src_ref=src, dst_ref=dst, send_sem=ssem, recv_sem=rsem,
            device_id=(dev, 0), device_id_type=pl.DeviceIdType.MESH,
        )

    barrier = pltpu.get_barrier_semaphore()

    def greet(dev):
        pl.semaphore_signal(
            barrier, inc=1, device_id=(dev, 0), device_id_type=pl.DeviceIdType.MESH
        )

    loads = [
        pltpu.make_async_copy(src, dst, w_sem.at[i])
        for i, (src, dst) in enumerate(
            [(sup_hbm, sup), (sdown_hbm, sdown), (up_hbm.at[0], up), (down_hbm.at[0], down)]
        )
    ]
    loads[0].start()
    loads[2].start()
    loads[3].start()
    loads[1].start()
    for dev in (sib, n1, n2):
        greet(dev)

    @pl.when(z > 0)
    def _():
        greet(below)

    @pl.when(z < lines - 1)
    def _():
        greet(above)

    slot_count = chips * 2
    replicas = slot_count // 8
    spans = len_ref.shape[1]
    span = rows // spans
    row_at = lax.broadcasted_iota(jnp.int32, (rows, spans), 0)
    start_at = lax.broadcasted_iota(jnp.int32, (rows, spans), 1) * span
    lane_at = lax.broadcasted_iota(jnp.int32, (rows, EXTRA), 1).astype(F32)
    square = (rows, rows)
    diagonal = lax.broadcasted_iota(jnp.int32, square, 0) == lax.broadcasted_iota(
        jnp.int32, square, 1
    )
    for s in range(steps):
        lens = jnp.minimum(len_ref[pl.ds(s, 1), :], span)
        inside = (row_at >= start_at) & (row_at < start_at + lens)
        alive = jnp.sum(jnp.where(inside, 1.0, 0.0), axis=1, keepdims=True)
        ids = ids_ref[s]
        moved = (ids < replicas) & (second_ref[s] == 1)
        slot = jnp.where(moved, ids + (slot_count - replicas), ids).astype(F32)
        weights = gain_ref[s]
        dense = jnp.zeros((rows, EXTRA), F32)
        for k in range(ids.shape[0]):
            named = jnp.where(diagonal, slot[k : k + 1, :], 0.0)
            heavy = jnp.where(diagonal, weights[k : k + 1, :], 0.0)
            named = jnp.sum(named, axis=1, keepdims=True)
            heavy = jnp.sum(heavy, axis=1, keepdims=True)
            dense = dense + jnp.where(lane_at == named, heavy, 0.0)
        dense = dense * alive
        high = dense.astype(BF)
        x_ref[0, s, :, :half] = own_ref[s, :, :half]
        x_ref[1, s, :, :half] = own_ref[s, :, half:]
        x_ref[0, s, :, half:] = high
        x_ref[1, s, :, half:] = (dense - high.astype(F32)).astype(BF)
        live_ref[s] = jnp.broadcast_to(alive, (rows, 128))

    pl.semaphore_wait(barrier, 3 + jnp.minimum(z, 1) + jnp.minimum(lines - 1 - z, 1))

    def swap(s):
        return send(
            x_ref.at[1 - c, s], gat.at[1 - c, s, chip, c], swap_s.at[s], swap_r.at[s], sib
        )

    def block(s, who):
        return gat.at[c, s, who]

    def go_up(s, zz):
        b = block(s, chip_of(zz, d1, d2))
        return send(b, b, zu_s.at[s, zz], ag_r.at[s, chip_of(zz, d1, d2)], above)

    def go_dn(s, zz):
        b = block(s, chip_of(zz, d1, d2))
        return send(b, b, zd_s.at[s, zz], ag_r.at[s, chip_of(zz, d1, d2)], below)

    def go_d1(s, zz):
        b = block(s, chip_of(zz, d1, d2))
        return send(b, b, d1_s.at[s, zz], ag_r.at[s, chip_of(zz, d1, d2)], n1)

    def go_d2(s, a, zz):
        b = block(s, chip_of(zz, a, d2))
        return send(b, b, d2_s.at[s, a * lines + zz], ag_r.at[s, chip_of(zz, a, d2)], n2)

    def go_sib(s, who):
        b = block(s, who)
        return send(b, b, sib_s.at[s, who], sib_r.at[s, who], sib)

    def arrived(s, who):
        b = block(s, who)
        send(b, b, sib_s.at[s, who], ag_r.at[s, who], sib).wait_recv()

    def spread(s, zz):
        go_d1(s, zz).start()
        go_d2(s, d1, zz).start()
        go_sib(s, chip_of(zz, d1, d2)).start()

    def ag_own(s):
        swap(s).wait_recv()

        @pl.when(z < lines - 1)
        def _():
            go_up(s, z).start()

        @pl.when(z > 0)
        def _():
            go_dn(s, z).start()

    def ag_line(s, d):
        @pl.when(z - d >= 0)
        def _():
            arrived(s, chip_of(z - d, d1, d2))

            @pl.when(z < lines - 1)
            def _():
                go_up(s, z - d).start()

            if s == 0:
                spread(s, z - d)

        @pl.when(z + d < lines)
        def _():
            arrived(s, chip_of(z + d, d1, d2))

            @pl.when(z > 0)
            def _():
                go_dn(s, z + d).start()

            if s == 0:
                spread(s, z + d)

    def ag_d1(s, k):
        zz = order(k)
        arrived(s, chip_of(zz, 1 - d1, d2))
        go_d2(s, 1 - d1, zz).start()
        go_sib(s, chip_of(zz, 1 - d1, d2)).start()

    def ag_d2(s, m):
        a = (d1 + m // lines) % 2
        who = chip_of(order(m % lines), a, 1 - d2)
        arrived(s, who)
        go_sib(s, who).start()

    def loop(n, body):
        def step(i, carry):
            body(i)
            return carry

        lax.fori_loop(0, n, step, 0)

    def ag_finish(s):
        def one(who):
            b = gat.at[1 - c, s, who]
            send(b, b, sib_s.at[s, who], sib_r.at[s, who], sib).wait_recv()

        loop(chips, one)

    def cut(i, n):
        return pl.ds(pl.multiple_of(i * n, n), n)

    def shared_up_chunk(i):
        cols = cut(i, 256)
        v = mm(x_ref[0, :, :, :half].reshape(steps * rows, half), sup[:half, cols])
        v = v + mm(x_ref[1, :, :, :half].reshape(steps * rows, half), sup[half:, cols])
        shid[:, cols] = silu(v).astype(BF)

    def shared_down_chunk(j):
        cols = cut(j, 512)
        shout[:, cols] = mm(shid[...], sdown[:, cols])

    def gains(s):
        lane = lax.broadcasted_iota(jnp.int32, (chips * 2 * rows, EXTRA), 1)
        both = gat[0, s, :, :, :, half:].astype(F32) + gat[1, s, :, :, :, half:].astype(F32)
        both = both.reshape(chips * 2 * rows, EXTRA)
        mine = jnp.sum(jnp.where(lane == me, both, 0.0), axis=1, keepdims=True)
        gain[...] = mine.reshape(chips, 2 * rows, 1)

    def up_chunk(s, i):
        cols = cut(i, 256)
        v = mm(gat[0, s, :, :, :, :half].reshape(chips * 2 * rows, half), up[:half, cols])
        v = v + mm(gat[1, s, :, :, :, :half].reshape(chips * 2 * rows, half), up[half:, cols])
        hid[:, :, cols] = silu(v).astype(BF).reshape(chips, 2 * rows, 256)

    def members(t, far):
        there = y + t * (x - y)
        b = (1 - there) if far else there
        return [
            zz * 4 + a * (1 + t) + b * (2 - t) for zz in range(lines) for a in range(2)
        ]

    def down_chunk(s, t, far, j):
        group = members(t, far)
        source = jnp.concatenate([hid[who] for who in group], axis=0)
        scale = jnp.concatenate([gain[who] for who in group], axis=0)
        v = mm(source, down[:, pl.ds(pl.multiple_of(t * half + j * 256, 256), 256)])
        v = (v * scale).astype(BF).reshape(len(group), 2, rows, 256)
        for i, who in enumerate(group):
            part[t, s, who, :, :, cut(j, 256)] = v[i]

    def x0(s, who):
        return send(
            part.at[1 - c, s, who], swapped.at[s, who], x0_s.at[s, who], x0_r.at[s, who], sib
        )

    def x0_start(s, far):
        for who in members(1 - c, far):
            x0(s, who).start()

    def both_cores(s, who):
        x0(s, who).wait_recv()
        return part[c, s, who].astype(F32) + swapped[s, who].astype(F32)

    def f_copy(s, a, zz):
        who = chip_of(zz, a, 1 - d2)
        i = a * lines + zz
        return send(part.at[c, s, who], from_f.at[s, i], f_s.at[s, i], f_r.at[s, i], n2)

    def rs_f(s, q):
        a = (1 - d1 + q // lines) % 2
        zz = order(q % lines)
        who = chip_of(zz, a, 1 - d2)
        part[c, s, who] = both_cores(s, who).astype(BF)
        f_copy(s, a, zz).start()

    def with_f(s, a, zz):
        f_copy(s, a, zz).wait_recv()
        who = chip_of(zz, a, d2)
        return both_cores(s, who) + from_f[s, a * lines + zz].astype(F32)

    def s_copy(s, zz):
        who = chip_of(zz, 1 - d1, d2)
        return send(part.at[c, s, who], from_s.at[s, zz], s_s.at[s, zz], s_r.at[s, zz], n1)

    def rs_s(s, k):
        zz = order(k)
        who = chip_of(zz, 1 - d1, d2)
        part[c, s, who] = with_f(s, 1 - d1, zz).astype(BF)
        s_copy(s, zz).start()

    def up_copy(s, zz):
        who = chip_of(zz, d1, d2)
        return send(part.at[c, s, who], from_up.at[s, zz], ru_s.at[s, zz], ru_r.at[s, zz], above)

    def dn_copy(s, zz):
        who = chip_of(zz, d1, d2)
        return send(part.at[c, s, who], from_dn.at[s, zz], rd_s.at[s, zz], rd_r.at[s, zz], below)

    def rs_collect(s):
        def collect(k):
            zz = order(k)
            who = chip_of(zz, d1, d2)
            v = with_f(s, d1, zz)
            s_copy(s, zz).wait_recv()
            part[c, s, who] = (v + from_s[s, zz].astype(F32)).astype(BF)

        loop(lines, collect)

    def rs_hop(s, d):
        @pl.when(z + d < lines)
        def _():
            zz = z + d
            who = chip_of(zz, d1, d2)

            @pl.when(z > 0)
            def _():
                up_copy(s, zz).wait_recv()
                v = part[c, s, who].astype(F32) + from_up[s, zz].astype(F32)
                part[c, s, who] = v.astype(BF)

            up_copy(s, zz).start()

        @pl.when(z - d >= 0)
        def _():
            zz = z - d
            who = chip_of(zz, d1, d2)

            @pl.when(z < lines - 1)
            def _():
                dn_copy(s, zz).wait_recv()
                v = part[c, s, who].astype(F32) + from_dn[s, zz].astype(F32)
                part[c, s, who] = v.astype(BF)

            dn_copy(s, zz).start()

    def fin(s):
        return send(part.at[c, s, chip, 1 - c], from_fin.at[s], fin_s.at[s], fin_r.at[s], sib)

    def rs_own(s):
        @pl.when(z > 0)
        def _():
            up_copy(s, z).wait_recv()
            v = part[c, s, chip].astype(F32) + from_up[s, z].astype(F32)
            part[c, s, chip] = v.astype(BF)

        @pl.when(z < lines - 1)
        def _():
            dn_copy(s, z).wait_recv()
            v = part[c, s, chip].astype(F32) + from_dn[s, z].astype(F32)
            part[c, s, chip] = v.astype(BF)

        fin(s).start()

    def write(s):
        fin(s).wait_recv()
        keep = part[c, s, chip, c].astype(F32)
        other = from_fin[s].astype(F32)
        lead = jnp.where(c == 0, keep, other)
        tail = jnp.where(c == 0, other, keep)
        alive = live_ref[s, :, :1]
        mine = pl.ds(s * rows, rows)
        out_ref[s, :, :half] = ((lead + shout[mine, :half]) * alive).astype(out_ref.dtype)
        out_ref[s, :, half:] = ((tail + shout[mine, half:]) * alive).astype(out_ref.dtype)

    for s in range(steps):
        gat[c, s, chip, c] = x_ref[c, s]
        swap(s).start()
    ag_own(0)
    spread(0, z)
    ag_own(1)
    for d in range(1, lines):
        ag_line(0, d)
        ag_line(1, d)
        if d < lines - 1:
            ag_d1(0, d - 1)
    loads[0].wait()

    def first(k):
        shared_up_chunk(k)

        @pl.when(k < 2)
        def _():
            ag_d1(0, k + lines - 2)

    loop(lines, first)
    loop(lines, lambda k: spread(1, order(k)))
    loop(2 * lines, lambda m: ag_d2(0, m))
    ag_finish(0)
    loads[2].wait()
    gains(0)

    def third(i):
        up_chunk(0, i)
        ag_d1(1, i)

    loop(hidden_units // 256, third)
    loads[3].wait()
    chunks = half // 256
    late = chunks - lines
    loop(chunks, lambda j: down_chunk(0, 1 - c, True, j))
    x0_start(0, True)
    loop(chunks, lambda j: down_chunk(0, c, True, j))
    loop(2 * lines, lambda q: rs_f(0, q))

    def fourth(j):
        down_chunk(0, 1 - c, False, j)

        @pl.when(j >= late)
        def _():
            ag_d2(1, j - late)

    loop(chunks, fourth)
    x0_start(0, False)

    def fifth(j):
        down_chunk(0, c, False, j)

        @pl.when(j >= late)
        def _():
            ag_d2(1, j - late + lines)

    loop(chunks, fifth)
    ag_finish(1)
    gains(1)
    loop(hidden_units // 256, lambda i: up_chunk(1, i))

    def sixth(j):
        down_chunk(1, 1 - c, True, j)

        @pl.when(j >= late)
        def _():
            rs_s(0, j - late)

    loop(chunks, sixth)
    x0_start(1, True)
    loop(chunks, lambda j: down_chunk(1, c, True, j))
    loop(2 * lines, lambda q: rs_f(1, q))
    rs_collect(0)
    rs_hop(0, 3)
    loop(chunks, lambda j: down_chunk(1, 1 - c, False, j))
    x0_start(1, False)
    rs_hop(0, 2)
    loop(chunks, lambda j: down_chunk(1, c, False, j))
    rs_hop(0, 1)
    loop(lines, lambda k: rs_s(1, k))
    loads[1].wait()
    loop(3, shared_down_chunk)
    rs_own(0)
    rs_collect(1)
    rs_hop(1, 3)
    loop(2, lambda j: shared_down_chunk(3 + j))
    rs_hop(1, 2)
    loop(2, lambda j: shared_down_chunk(5 + j))
    rs_hop(1, 1)
    write(0)
    rs_own(1)
    write(1)

    for s in range(steps):
        swap(s).wait_send()
        fin(s).wait_send()

        def planes(zz):
            go_d1(s, zz).wait_send()
            go_d2(s, 0, zz).wait_send()
            go_d2(s, 1, zz).wait_send()
            f_copy(s, 0, zz).wait_send()
            f_copy(s, 1, zz).wait_send()
            s_copy(s, zz).wait_send()

            @pl.when((zz <= z) & (z < lines - 1))
            def _():
                go_up(s, zz).wait_send()

            @pl.when((zz >= z) & (z > 0))
            def _():
                go_dn(s, zz).wait_send()

            @pl.when(zz > z)
            def _():
                up_copy(s, zz).wait_send()

            @pl.when(zz < z)
            def _():
                dn_copy(s, zz).wait_send()

        loop(lines, planes)

        def siblings(who):
            go_sib(s, who).wait_send()
            x0(s, who).wait_send()

        loop(chips, siblings)


def fused_layer(
    hidden_rows, draft_len, expert_ids, replica, route_gain, slot_up, slot_down, shared_up, shared_down
):
    slot_count = lax.axis_size("expert")
    steps, rows, width = hidden_rows.shape
    half = width // 2
    chips = slot_count // 2
    lines = chips // 4
    hidden_units = slot_up.shape[2]
    vm = pl.BlockSpec(memory_space=pltpu.VMEM)
    hbm = pl.BlockSpec(memory_space=pl.ANY)
    dma = pltpu.SemaphoreType.DMA
    flops = 4 * steps * rows * (slot_count + 1) * width * hidden_units
    return pl.pallas_call(
        fused,
        out_shape=jax.ShapeDtypeStruct((steps, rows, width), BF),
        in_specs=[vm] * 5 + [hbm] * 4,
        out_specs=vm,
        scratch_shapes=[
            pltpu.VMEM((2, steps, rows, half + EXTRA), BF),
            pltpu.VMEM((steps, rows, 128), F32),
            pltpu.VMEM((2, steps, chips, 2, rows, half + EXTRA), BF),
            pltpu.VMEM((2, steps, chips, 2, rows, half), BF),
            pltpu.VMEM((steps, chips, 2, rows, half), BF),
            pltpu.VMEM((steps, 2 * lines, 2, rows, half), BF),
            pltpu.VMEM((steps, lines, 2, rows, half), BF),
            pltpu.VMEM((steps, lines, 2, rows, half), BF),
            pltpu.VMEM((steps, lines, 2, rows, half), BF),
            pltpu.VMEM((steps, rows, half), BF),
            pltpu.VMEM(slot_up.shape[1:], BF),
            pltpu.VMEM(slot_down.shape[1:], BF),
            pltpu.VMEM(shared_up.shape, BF),
            pltpu.VMEM(shared_down.shape, BF),
            pltpu.VMEM((chips, 2 * rows, hidden_units), BF),
            pltpu.VMEM((chips, 2 * rows, 1), F32),
            pltpu.VMEM((steps * rows, shared_up.shape[1]), BF),
            pltpu.VMEM((steps * rows, width), F32),
            dma((4,)), dma((steps,)), dma((steps,)),
            dma((steps, lines)), dma((steps, lines)), dma((steps, lines)),
            dma((steps, 2 * lines)), dma((steps, chips)),
            dma((steps, chips)), dma((steps, chips)),
            dma((steps, chips)), dma((steps, chips)),
            dma((steps, 2 * lines)), dma((steps, 2 * lines)),
            dma((steps, lines)), dma((steps, lines)),
            dma((steps, lines)), dma((steps, lines)),
            dma((steps, lines)), dma((steps, lines)),
            dma((steps,)), dma((steps,)),
        ],
        compiler_params=pltpu.CompilerParams(
            collective_id=0, has_side_effects=True, vmem_limit_bytes=62 * 1024 * 1024
        ),
        cost_estimate=pl.CostEstimate(
            flops=flops, bytes_accessed=4 * 2 * width * hidden_units, transcendentals=0
        ),
        name="fused_layer",
    )(
        hidden_rows, draft_len, jnp.swapaxes(expert_ids, 1, 2), jnp.swapaxes(replica, 1, 2),
        jnp.swapaxes(route_gain, 1, 2), slot_up, slot_down, shared_up, shared_down,
    )


def slot_gains(lengths, chosen, second, gains, slot_count):
    row_count = chosen.shape[1]
    span = row_count // lengths.shape[1]
    replicas = slot_count // 8
    experts_all = slot_count - replicas
    limit = jnp.repeat(lengths, span, axis=1, total_repeat_length=row_count)
    live = (jnp.arange(row_count, dtype=jnp.int32)[None] % span < limit).astype(jnp.float32)
    slot = jnp.where((chosen < replicas) & (second == 1), chosen + experts_all, chosen)
    hit = slot[..., None] == jnp.arange(slot_count, dtype=jnp.int32)
    dense = jnp.sum(jnp.where(hit, gains[..., None], 0.0), axis=2)
    return live, dense * live[..., None]


def shards(
    hidden_rows,
    draft_len,
    expert_ids,
    replica,
    route_gain,
    slot_up,
    slot_down,
    shared_up,
    shared_down,
):
    slot_count = lax.axis_size("expert")
    me = lax.axis_index("expert")
    steps, rows, _ = hidden_rows.shape
    own = lax.all_gather(hidden_rows, "tensor", axis=2, tiled=True)
    width = own.shape[2]
    live, dense = slot_gains(draft_len, expert_ids, replica, route_gain, slot_count)
    high = dense.astype(jnp.bfloat16)
    low = (dense - high.astype(jnp.float32)).astype(jnp.bfloat16)
    packed = jnp.concatenate([own, high, low], axis=2)
    routed = []
    for index in range(steps):
        everything = lax.all_gather(packed[index], "expert", axis=0, tiled=True)
        source = everything[:, :width]
        pick = jnp.arange(slot_count) == me
        both = everything[:, width:].astype(jnp.float32)
        both = both[:, :slot_count] + both[:, slot_count:]
        weight = jnp.sum(jnp.where(pick[None], both, 0.0), axis=1, keepdims=True)
        hidden = jax.nn.silu(
            jnp.dot(source, slot_up[0], preferred_element_type=jnp.float32)
        ).astype(jnp.bfloat16)
        part = jnp.dot(hidden, slot_down[0], preferred_element_type=jnp.float32)
        part = (part * weight).astype(jnp.bfloat16)
        part = lax.psum_scatter(part, "tensor", scatter_dimension=1, tiled=True)
        routed.append(lax.psum_scatter(part, "expert", scatter_dimension=0, tiled=True))
    flat = own.reshape(steps * rows, width)
    shared_act = jax.nn.silu(
        jnp.dot(flat, shared_up, preferred_element_type=jnp.float32)
    ).astype(jnp.bfloat16)
    shared_out = jnp.dot(shared_act, shared_down, preferred_element_type=jnp.float32)
    if lax.axis_size("tensor") > 1:
        shared_out = lax.psum_scatter(shared_out, "tensor", scatter_dimension=1, tiled=True)
    shared_out = shared_out.reshape(steps, rows, -1)
    total = jnp.stack(routed).astype(jnp.float32) + shared_out
    return (total * live[..., None]).astype(jnp.bfloat16)


def solution(mesh):
    fits = mesh.shape["tensor"] == 1 and mesh.shape["expert"] == 32
    return jax.shard_map(
        fused_layer if fits else shards,
        mesh=mesh,
        in_specs=(
            P(None, "expert", "tensor"),
            P(None, "expert"),
            P(None, "expert", None),
            P(None, "expert", None),
            P(None, "expert", None),
            P("expert", None, "tensor"),
            P("expert", "tensor", None),
            P(None, "tensor"),
            P("tensor", None),
        ),
        out_specs=P(None, "expert", "tensor"),
        check_vma=False,
    )
```
